32 devices in a mesh: ti: 8 (over z, x), kz: 4 (over y, core).
Axes of the slice: x: 2, y: 2, z: 4, core: 2. Of those that a mesh axis runs over, the one named last changes fastest.
Arguments:
- point_maps: float32 [3, 4, 160, 256], P(None, None, 'kz'), may hold values from 0.3 to 3, as said below
- point_coils: float32 [2, 8, 4, 160, 256], P(None, None, None, 'kz'), may hold values from -2 to 2
- direction_maps: float32 [3, 4, 160, 256], P(None, None, 'kz', 'ti'), may hold values from -12 to 12
- direction_coils: float32 [2, 8, 4, 160, 256], P(None, None, None, 'kz', 'ti'), may hold values from -12 to 12
- residual_maps: float32 [3, 4, 160, 256], P(None, None, 'kz', 'ti'), may hold values from -12 to 12
- residual_coils: float32 [2, 8, 4, 160, 256], P(None, None, None, 'kz', 'ti'), may hold values from -12 to 12
- inversion_times: float32 [16], P('ti'), may hold values from 0.05 to 3
- sampling_mask: int32 [16, 160, 256], P('ti'), may hold values 0 or 1
Outputs:
- new_residual_maps: float32 [3, 4, 160, 256], P(None, None, 'kz', 'ti')
- new_residual_coils: float32 [2, 8, 4, 160, 256], P(None, None, None, 'kz', 'ti')
- new_direction_maps: float32 [3, 4, 160, 256], P(None, None, 'kz', 'ti')
- new_direction_coils: float32 [2, 8, 4, 160, 256], P(None, None, None, 'kz', 'ti')
The draws below stay inside these ranges and needn't reach their ends.
Inputs may be any that keep to these rules, and one draw needn't show every extreme that they name: `sampling_mask`: 1 where the sample of that bin was acquired. `point_maps`: component 1 lies between 1.4 and 2 times component 0.
All inputs are finite; a program needn't handle non-finite values. No bound on the sum of `sampling_mask` on one device may be relied on, other than what follows from the above.
Results may differ from the reference program's by a relative error of at most 0.0003.
Values sent between devices are 32-bit elements; how exact they have to be, the bound alone decides.
A program may use at most 128 MiB of HBM per device.

```python
import math
import jax
import jax.numpy as jnp
from jax import lax

COILS = 8
NY = 256
NZ = 160
BINS = 16
XS = 4


def ramp_scale(shape, power):
    zcoord = lax.broadcasted_iota(jnp.float32, shape, len(shape) - 2) / shape[-2]
    ycoord = lax.broadcasted_iota(jnp.float32, shape, len(shape) - 1) / shape[-1]
    return 10.0 ** (power * (zcoord + ycoord))


def drawn_field(key, shape):
    noise = jax.random.truncated_normal(key, -4.0, 4.0, shape, jnp.float32)
    return noise * ramp_scale(shape, 0.5) * 0.3


def draw_point_maps(key, part):
    key = jax.random.fold_in(key, 21)
    first_key, second_key, third_key = jax.random.split(key, 3)
    shape = (XS, NZ, NY)
    density = jax.random.uniform(first_key, shape, jnp.float32, 0.5, 1.5)
    amplitude = density * jax.random.uniform(second_key, shape, jnp.float32, 1.4, 2.0)
    relax_rate = jnp.exp(jax.random.uniform(third_key, shape, jnp.float32, jnp.log(0.3), jnp.log(3.0)))
    return jnp.stack([density, amplitude, relax_rate])


def draw_direction_maps(key, part):
    key = jax.random.fold_in(key, 31)
    return drawn_field(key, (3, XS, NZ, NY))


def draw_direction_coils(key, part):
    key = jax.random.fold_in(key, 41)
    return drawn_field(key, (2, COILS, XS, NZ, NY))


def draw_residual_maps(key, part):
    key = jax.random.fold_in(key, 51)
    return drawn_field(key, (3, XS, NZ, NY))


def draw_residual_coils(key, part):
    key = jax.random.fold_in(key, 61)
    return drawn_field(key, (2, COILS, XS, NZ, NY))


def with_ends(values, key, low, largest):
    longest = values.shape.index(max(values.shape))
    spots = []
    for shift in (0, 1):
        where = [jax.random.randint(jax.random.fold_in(key, axis), (), 0, length) for axis, length in enumerate(values.shape)]
        where[longest] = (where[longest] + shift) % values.shape[longest]
        spots.append(tuple(where))
    return values.at[spots[0]].set(low).at[spots[1]].set(largest)


def level_of(stream_key, extent, cuts, low, top_value):
    level, own = 1.0, jax.random.fold_in(stream_key, 6)
    for position, parts in cuts:
        draws = jnp.exp(jax.random.uniform(jax.random.fold_in(own, position), (parts,), jnp.float32, low / len(cuts), top_value / len(cuts)))
        level = level * jnp.repeat(draws, extent[position] // parts).reshape([-1 if axis == position else 1 for axis in range(len(extent))])
    return level


def normal_values(key, dims, width, limit, pieces=(), dtype=jnp.bfloat16):
    values = width * jax.random.normal(key, dims, jnp.float32)
    if pieces:
        values = values * level_of(key, dims, pieces, -0.22, 0.18)
    return jnp.clip(values, -limit, limit).astype(dtype)


def setup_inputs(seed: int = 0) -> dict:
    streams_of = jax.random.split(jax.random.key(seed), 9)
    point_maps = draw_point_maps(jax.random.fold_in(streams_of[8], 71), 0)
    point_coils = normal_values(streams_of[1], (2, COILS, XS, NZ, NY), 0.35, 2.0, ((3, 4),), jnp.float32)
    direction_maps = draw_direction_maps(jax.random.fold_in(streams_of[8], 71), 0)
    direction_coils = draw_direction_coils(jax.random.fold_in(streams_of[8], 71), 0)
    residual_maps = draw_residual_maps(jax.random.fold_in(streams_of[8], 71), 0)
    residual_coils = draw_residual_coils(jax.random.fold_in(streams_of[8], 71), 0)
    inversion_times = jnp.clip(jnp.exp(math.log(3.0) - 4.0943445 * jax.random.uniform(streams_of[6], (BINS,), jnp.float32) ** level_of(streams_of[6], (BINS,), ((0, 8),), -0.2, 0.2)), 0.05, 3.0)
    sampling_mask = with_ends((jax.random.randint(streams_of[7], (BINS, NZ, NY), 0, 3) < 1).astype(jnp.int32), jax.random.fold_in(streams_of[7], 1), 0, 1)
    return {"point_maps": point_maps, "point_coils": point_coils, "direction_maps": direction_maps, "direction_coils": direction_coils, "residual_maps": residual_maps, "residual_coils": residual_coils, "inversion_times": inversion_times, "sampling_mask": sampling_mask}


regular_weight = 2.0


def reference(point_maps, point_coils, direction_maps, direction_coils, residual_maps, residual_coils, inversion_times, sampling_mask):
    density = point_maps[0]
    amplitude = point_maps[1]
    relax_rate = point_maps[2]
    coil_map = point_coils[0] + 1j * point_coils[1]
    coil_step = direction_coils[0] + 1j * direction_coils[1]

    def per_bin(totals, inputs):
        bin_time, bin_mask = inputs
        decays = jnp.exp(-bin_time * relax_rate)
        signal = density - amplitude * decays
        signal_step = direction_maps[0] - direction_maps[1] * decays + amplitude * bin_time * decays * direction_maps[2]
        images = coil_map * signal_step[None] + coil_step * signal[None]
        kspace = jnp.fft.fft2(images, axes=(-2, -1), norm="ortho") * bin_mask.astype(jnp.float32)[None, None]
        returned = jnp.fft.ifft2(kspace, axes=(-2, -1), norm="ortho")
        back_re = jnp.real(returned)
        back_im = jnp.imag(returned)
        projected = jnp.sum(point_coils[0] * back_re + point_coils[1] * back_im, axis=0)
        g_density, g_amplitude, g_rate, g_real, g_imag = totals
        return (g_density + projected,
                g_amplitude - decays * projected,
                g_rate + amplitude * bin_time * decays * projected,
                g_real + signal[None] * back_re,
                g_imag + signal[None] * back_im), None

    zero_map = jnp.zeros(density.shape, jnp.float32)
    zero_coil = jnp.zeros(point_coils.shape[1:], jnp.float32)
    totals, unused = lax.scan(per_bin, (zero_map, zero_map, zero_map, zero_coil, zero_coil), (inversion_times, sampling_mask))
    applied_maps = jnp.stack([totals[0], totals[1], totals[2]]) + regular_weight * direction_maps
    applied_coils = jnp.stack([totals[3], totals[4]]) + regular_weight * direction_coils
    old_norm = jnp.sum(residual_maps * residual_maps) + jnp.sum(residual_coils * residual_coils)
    curvature = jnp.sum(direction_maps * applied_maps) + jnp.sum(direction_coils * applied_coils)
    step_size = old_norm / curvature
    new_residual_maps = residual_maps - step_size * applied_maps
    new_residual_coils = residual_coils - step_size * applied_coils
    new_norm = jnp.sum(new_residual_maps * new_residual_maps) + jnp.sum(new_residual_coils * new_residual_coils)
    conjugacy = new_norm / old_norm
    new_direction_maps = new_residual_maps + conjugacy * direction_maps
    new_direction_coils = new_residual_coils + conjugacy * direction_coils
    return new_residual_maps, new_residual_coils, new_direction_maps, new_direction_coils
```

```python
import functools
import math

import jax
import jax.numpy as jnp
import ml_dtypes
import numpy as np
from jax import lax
from jax.experimental import pallas as pl
from jax.experimental.pallas import tpu as pltpu
from jax.sharding import PartitionSpec as P

MESH = pl.DeviceIdType.MESH
regular_weight = 2.0
COIL_GROUPS = 4
LANES = 128
VMEM_LIMIT = 48 * 1024 * 1024


def split_table(table):
    high = table.astype(ml_dtypes.bfloat16)
    low = (table - high.astype(np.float64)).astype(ml_dtypes.bfloat16)
    return np.stack([high, low])


def dft_parts(length):
    indices = np.arange(length)
    angles = (indices[:, None] * indices[None, :] % length) * (2.0 * math.pi / length)
    factor = 1.0 / math.sqrt(length)
    return np.cos(angles) * factor, np.sin(angles) * factor


def tables_y(length):
    c, s = dft_parts(length)
    forward = np.block([[c, -s], [s, c]])
    backward = np.block([[c, s], [-s, c]])
    return split_table(forward), split_table(backward)


def tables_z(length):
    c, s = dft_parts(length)
    forward = np.block([[c, s], [-s, c]])
    backward = np.block([[c, -s], [s, c]])
    return split_table(forward), split_table(backward)


def halves(values):
    high = values.astype(jnp.bfloat16)
    low = (values - high.astype(jnp.float32)).astype(jnp.bfloat16)
    return high, low


dot = functools.partial(jnp.dot, preferred_element_type=jnp.float32)


def from_right(values, table):
    high, low = halves(values)
    return dot(high, table[0]) + (dot(low, table[0]) + dot(high, table[1]))


def from_left(table, values):
    high, low = halves(values)
    return dot(table[0], high) + (dot(table[0], low) + dot(table[1], high))


def packed_coils(coils, x, group, per_group):
    parts = [coils[ri, group * per_group + c, x] for c in range(per_group) for ri in range(2)]
    return wide(jnp.concatenate(parts, axis=-1))


def packed_maps(maps, x):
    parts = [maps[m, x] for m in range(3)]
    return wide(jnp.concatenate(parts + [jnp.zeros_like(parts[0])], axis=-1))


def wide(values):
    missing = LANES - values.shape[-1]
    if missing:
        values = jnp.concatenate([values, jnp.zeros((values.shape[0], missing), values.dtype)], axis=-1)
    return values


def enter(n_ti, n_kz, me):
    total = n_ti * n_kz
    barrier = pltpu.get_barrier_semaphore()

    def greet(offset, carry):
        other = lax.rem(me + offset, total)
        pl.semaphore_signal(
            barrier, inc=1, device_id=(other // n_kz, lax.rem(other, n_kz)), device_id_type=MESH
        )
        return carry

    lax.fori_loop(1, total, greet, 0)
    return barrier


def gather_kernel(
    n_ti, n_kz, per_group,
    dir_maps, dir_coils, maps, coils, times, mask,
    got_dir, got_maps, got_coils, got_times, got_mask,
    send, dir_out, dir_in, map_out, map_in, coil_out, coil_in, time_out, time_in, mask_out, mask_in, own,
):
    total = n_ti * n_kz
    ti = lax.axis_index("ti")
    kz = lax.axis_index("kz")
    me = ti * n_kz + kz
    group = lax.rem(ti, COIL_GROUPS)
    first = (ti // COIL_GROUPS) * COIL_GROUPS
    barrier = enter(n_ti, n_kz, me)

    my_coils = pl.ds(group * per_group, per_group)
    locals_ = [
        pltpu.make_async_copy(maps.at[:, kz], got_maps.at[kz], own.at[0]),
        pltpu.make_async_copy(coils.at[:, my_coils, kz], got_coils.at[kz], own.at[1]),
        pltpu.make_async_copy(times, got_times.at[group], own.at[2]),
        pltpu.make_async_copy(mask, got_mask.at[group], own.at[3]),
    ]
    for copy in locals_:
        copy.start()

    for x in range(n_kz):
        packed = packed_maps(dir_maps, x)
        for g in range(COIL_GROUPS):
            send[x, g, 0] = packed_coils(dir_coils, x, g, per_group)
            send[x, g, 1] = packed
    own_dir = pltpu.make_async_copy(send.at[kz, group], got_dir.at[me], own.at[4])
    own_dir.start()

    pl.semaphore_wait(barrier, total - 1)

    def mask_copies(other, slot, sem):
        where = (first + other, kz)
        return [
            pltpu.make_async_remote_copy(
                mask, got_mask.at[slot], mask_out.at[other], mask_in.at[sem], device_id=where, device_id_type=MESH
            ),
            pltpu.make_async_remote_copy(
                times, got_times.at[slot], time_out.at[other], time_in.at[sem], device_id=where, device_id_type=MESH
            ),
        ]

    def point_copies(other, slot, sem):
        where = (ti, other)
        return [
            pltpu.make_async_remote_copy(
                maps.at[:, other], got_maps.at[slot], map_out.at[other], map_in.at[sem],
                device_id=where, device_id_type=MESH,
            ),
            pltpu.make_async_remote_copy(
                coils.at[:, my_coils, other], got_coils.at[slot], coil_out.at[other], coil_in.at[sem],
                device_id=where, device_id_type=MESH,
            ),
        ]

    def dir_copy(other, slot, sem):
        other_ti = other // n_kz
        other_kz = lax.rem(other, n_kz)
        return pltpu.make_async_remote_copy(
            send.at[other_kz, lax.rem(other_ti, COIL_GROUPS)], got_dir.at[slot],
            dir_out.at[other], dir_in.at[sem],
            device_id=(other_ti, other_kz), device_id_type=MESH,
        )

    def send_dir(offset, carry):
        dir_copy(lax.rem(me + offset, total), me, me).start()
        return carry

    lax.fori_loop(1, total, send_dir, 0)
    for offset in range(1, n_kz):
        for copy in point_copies(lax.rem(kz + offset, n_kz), kz, kz):
            copy.start()
    for offset in range(1, COIL_GROUPS):
        for copy in mask_copies(lax.rem(group + offset, COIL_GROUPS), group, group):
            copy.start()

    for copy in locals_:
        copy.wait()
    own_dir.wait()

    def wait_dir(offset, carry):
        other = lax.rem(me + offset, total)
        copy = dir_copy(other, other, other)
        copy.wait_send()
        copy.wait_recv()
        return carry

    lax.fori_loop(1, total, wait_dir, 0)
    for offset in range(1, n_kz):
        other = lax.rem(kz + offset, n_kz)
        for copy in point_copies(other, other, other):
            copy.wait_send()
            copy.wait_recv()
    for offset in range(1, COIL_GROUPS):
        other = lax.rem(group + offset, COIL_GROUPS)
        for copy in mask_copies(other, other, other):
            copy.wait_send()
            copy.wait_recv()


def lane_block(width):
    return lambda rows: lax.broadcasted_iota(jnp.int32, (rows, LANES), 1) // width


def transform_kernel(
    n_ti, n_kz, per_group, bins,
    got_dir, got_maps, got_coils, times, mask, y_forward, y_backward, z_forward, z_backward,
    out, step_maps, step_coils, maps, coils, grad_maps, grad_coils,
):
    t = pl.program_id(0)
    rows = got_dir.shape[2]
    nz = maps.shape[1]
    width = maps.shape[2] // n_ti
    per_tile = LANES // width
    tiles = maps.shape[2] // LANES
    block_of = lax.broadcasted_iota(jnp.int32, (rows, LANES), 1) // width

    @pl.when(t == 0)
    def _():
        grad_maps[...] = jnp.zeros_like(grad_maps)
        grad_coils[...] = jnp.zeros_like(grad_coils)
        for k in range(n_kz):
            span = slice(k * rows, (k + 1) * rows)
            for m in range(3):
                maps[m, span, :] = got_maps[k, m]
            for c in range(per_group):
                for ri in range(2):
                    coils[2 * c + ri, span, :] = got_coils[k, ri, c]
            for h in range(tiles):
                lanes = slice(h * LANES, (h + 1) * LANES)
                for pack, target, planes in ((0, step_coils, 4), (1, step_maps, 3)):
                    blocks = [got_dir[(h * per_tile + j) * n_kz + k, pack] for j in range(per_tile)]
                    for p in range(planes):
                        value = blocks[p % per_tile]
                        value = jnp.zeros((rows, LANES), jnp.float32)
                        for j in range(per_tile):
                            shift = ((j - p) * width) % LANES
                            moved = pltpu.roll(blocks[j], shift, 1) if shift else blocks[j]
                            value = jnp.where(block_of == j, moved, value)
                        target[p, span, lanes] = value

    tau = times[0, 0, 0:1, 0:1]
    amplitude = maps[1]
    decays = jnp.exp(-tau * maps[2])
    signal = maps[0] - amplitude * decays
    slope = amplitude * tau * decays
    signal_step = step_maps[0] - step_maps[1] * decays + slope * step_maps[2]
    kept = mask[0, 0].astype(jnp.float32)

    along_y = []
    for c in range(per_group):
        real = coils[2 * c] * signal_step + step_coils[2 * c] * signal
        imag = coils[2 * c + 1] * signal_step + step_coils[2 * c + 1] * signal
        along_y.append(jnp.concatenate([real, imag], axis=1))
    ny = real.shape[1]
    both = from_right(jnp.concatenate(along_y, axis=0), y_forward)
    along_z = jnp.concatenate(
        [
            jnp.concatenate([both[c * nz : (c + 1) * nz, :ny], both[c * nz : (c + 1) * nz, ny:]], axis=0)
            for c in range(per_group)
        ],
        axis=1,
    )
    kspace = from_left(z_forward, along_z)
    kept_all = jnp.concatenate([jnp.concatenate([kept] * per_group, axis=1)] * 2, axis=0)
    back = from_left(z_backward, kspace * kept_all)
    both = jnp.concatenate(
        [
            jnp.concatenate([back[:nz, c * ny : (c + 1) * ny], back[nz:, c * ny : (c + 1) * ny]], axis=1)
            for c in range(per_group)
        ],
        axis=0,
    )
    back = from_right(both, y_backward)
    projected = jnp.zeros_like(signal)
    for c in range(per_group):
        real = back[c * nz : (c + 1) * nz, :ny]
        imag = back[c * nz : (c + 1) * nz, ny:]
        projected += coils[2 * c] * real + coils[2 * c + 1] * imag
        grad_coils[2 * c] += signal * real
        grad_coils[2 * c + 1] += signal * imag
    grad_maps[0] += projected
    grad_maps[1] -= decays * projected
    grad_maps[2] += slope * projected

    @pl.when(t == bins - 1)
    def _():
        for k in range(n_kz):
            span = slice(k * rows, (k + 1) * rows)
            for h in range(tiles):
                lanes = slice(h * LANES, (h + 1) * LANES)
                for pack, source, planes in ((0, grad_coils, 4), (1, grad_maps, 3)):
                    blocks = [source[p, span, lanes] for p in range(planes)]
                    for j in range(per_tile):
                        value = jnp.zeros((rows, LANES), jnp.float32)
                        for p in range(planes):
                            shift = ((p - j) * width) % LANES
                            moved = pltpu.roll(blocks[p], shift, 1) if shift else blocks[p]
                            value = jnp.where(block_of == p, moved, value)
                        out[(h * per_tile + j) * n_kz + k, pack] = value


def update_kernel(
    n_ti, n_kz, per_group,
    grads, dir_maps, dir_coils, res_maps, res_coils,
    new_res_maps, new_res_coils, new_dir_maps, new_dir_coils,
    got, direction, residual, applied, sums, got_sums,
    grad_out, grad_in, sum_out, sum_in, own,
):
    total = n_ti * n_kz
    ti = lax.axis_index("ti")
    kz = lax.axis_index("kz")
    me = ti * n_kz + kz
    barrier = enter(n_ti, n_kz, me)
    own_grad = pltpu.make_async_copy(grads.at[me], got.at[me], own.at[0])
    own_grad.start()
    pl.semaphore_wait(barrier, total - 1)

    def grad_copy(other, slot):
        return pltpu.make_async_remote_copy(
            grads.at[other], got.at[slot], grad_out.at[other], grad_in.at[slot],
            device_id=(other // n_kz, lax.rem(other, n_kz)), device_id_type=MESH,
        )

    def sum_copy(other, slot):
        return pltpu.make_async_remote_copy(
            sums, got_sums.at[slot], sum_out.at[other], sum_in.at[slot],
            device_id=(other // n_kz, lax.rem(other, n_kz)), device_id_type=MESH,
        )

    def send_grad(offset, carry):
        grad_copy(lax.rem(me + offset, total), me).start()
        return carry

    lax.fori_loop(1, total, send_grad, 0)

    for x in range(n_kz):
        for g in range(COIL_GROUPS):
            direction[x, g] = packed_coils(dir_coils, x, g, per_group)
            residual[x, g] = packed_coils(res_coils, x, g, per_group)
        direction[x, COIL_GROUPS] = packed_maps(dir_maps, x)
        residual[x, COIL_GROUPS] = packed_maps(res_maps, x)

    own_grad.wait()

    def wait_grad(offset, carry):
        other = lax.rem(me + offset, total)
        copy = grad_copy(other, other)
        copy.wait_send()
        copy.wait_recv()
        return carry

    lax.fori_loop(1, total, wait_grad, 0)

    zeros = jnp.zeros(got.shape[2:], jnp.float32)
    old, bend, cross, square = zeros, zeros, zeros, zeros
    for x in range(n_kz):
        for g in range(COIL_GROUPS + 1):
            if g < COIL_GROUPS:
                terms = [got[t * n_kz + x, 0] for t in range(g, n_ti, COIL_GROUPS)]
            else:
                terms = [got[t * n_kz + x, 1] for t in range(n_ti)]
            d = direction[x, g]
            r = residual[x, g]
            a = functools.reduce(lambda u, v: u + v, terms) + regular_weight * d
            applied[x, g] = a
            old += r * r
            bend += d * a
            cross += r * a
            square += a * a
    row = lax.broadcasted_iota(jnp.int32, sums.shape, 0)
    tile = jnp.zeros(sums.shape, jnp.float32)
    for i, part in enumerate((old, bend, cross, square)):
        tile = jnp.where(row == i, jnp.sum(part, keepdims=True), tile)
    sums[...] = tile

    def send_sum(offset, carry):
        sum_copy(lax.rem(me + offset, total), me).start()
        return carry

    lax.fori_loop(1, total, send_sum, 0)
    got_sums[me] = tile

    def wait_sum(offset, carry):
        other = lax.rem(me + offset, total)
        copy = sum_copy(other, other)
        copy.wait_send()
        copy.wait_recv()
        return carry

    lax.fori_loop(1, total, wait_sum, 0)
    whole = jnp.sum(got_sums[...], axis=0)
    old, bend, cross, square = (whole[i : i + 1, :] for i in range(4))
    step = old / bend
    ratio = (old - 2.0 * step * cross + step * step * square) / old
    width = dir_maps.shape[-1]
    for x in range(n_kz):
        for g in range(COIL_GROUPS + 1):
            r = residual[x, g] - step * applied[x, g]
            d = r + ratio * direction[x, g]
            for p in range(4 if g < COIL_GROUPS else 3):
                lanes = slice(p * width, (p + 1) * width)
                if g < COIL_GROUPS:
                    new_res_coils[p % 2, g * per_group + p // 2, x] = r[:, lanes]
                    new_dir_coils[p % 2, g * per_group + p // 2, x] = d[:, lanes]
                else:
                    new_res_maps[p, x] = r[:, lanes]
                    new_dir_maps[p, x] = d[:, lanes]


def shards(
    n_ti, n_kz,
    point_maps, point_coils, direction_maps, direction_coils,
    residual_maps, residual_coils, inversion_times, sampling_mask,
):
    total = n_ti * n_kz
    coils = point_coils.shape[1]
    per_group = coils // COIL_GROUPS
    rows, ny = point_maps.shape[2:]
    local_bins, nz, _ = sampling_mask.shape
    bins = COIL_GROUPS * local_bins
    f32 = jnp.float32
    any_ = pl.BlockSpec(memory_space=pl.ANY)
    vmem = pl.BlockSpec(memory_space=pltpu.VMEM)
    dma = pltpu.SemaphoreType.DMA
    times = jnp.broadcast_to(inversion_times[:, None, None], (local_bins, 8, LANES))

    got_dir, got_maps, got_coils, got_times, got_mask = pl.pallas_call(
        functools.partial(gather_kernel, n_ti, n_kz, per_group),
        out_shape=[
            jax.ShapeDtypeStruct((total, 2, rows, LANES), f32),
            jax.ShapeDtypeStruct((n_kz, 3, rows, ny), f32),
            jax.ShapeDtypeStruct((n_kz, 2, per_group, rows, ny), f32),
            jax.ShapeDtypeStruct((COIL_GROUPS,) + times.shape, f32),
            jax.ShapeDtypeStruct((COIL_GROUPS,) + sampling_mask.shape, jnp.int32),
        ],
        in_specs=[vmem, vmem, any_, any_, any_, any_],
        out_specs=[any_] * 5,
        scratch_shapes=[
            pltpu.VMEM((n_kz, COIL_GROUPS, 2, rows, LANES), f32),
            dma((total,)), dma((total,)),
            dma((n_kz,)), dma((n_kz,)), dma((n_kz,)), dma((n_kz,)),
            dma((COIL_GROUPS,)), dma((COIL_GROUPS,)), dma((COIL_GROUPS,)), dma((COIL_GROUPS,)),
            dma((5,)),
        ],
        compiler_params=pltpu.CompilerParams(
            collective_id=0, has_side_effects=True, vmem_limit_bytes=VMEM_LIMIT
        ),
        name="gather",
    )(direction_maps, direction_coils, point_maps, point_coils, times, sampling_mask)

    y_forward, y_backward = (jnp.asarray(t) for t in tables_y(ny))
    z_forward, z_backward = (jnp.asarray(t) for t in tables_z(nz))

    def whole(array):
        return pl.BlockSpec(array.shape, lambda t: (0,) * array.ndim)

    grads = pl.pallas_call(
        functools.partial(transform_kernel, n_ti, n_kz, per_group, bins),
        out_shape=jax.ShapeDtypeStruct((total, 2, rows, LANES), f32),
        grid=(bins,),
        in_specs=[
            whole(got_dir), whole(got_maps), whole(got_coils),
            pl.BlockSpec((1, 1, 8, LANES), lambda t: (t // local_bins, t % local_bins, 0, 0)),
            pl.BlockSpec((1, 1, nz, ny), lambda t: (t // local_bins, t % local_bins, 0, 0)),
            whole(y_forward), whole(y_backward), whole(z_forward), whole(z_backward),
        ],
        out_specs=pl.BlockSpec((total, 2, rows, LANES), lambda t: (0, 0, 0, 0)),
        scratch_shapes=[
            pltpu.VMEM((3, nz, ny), f32),
            pltpu.VMEM((2 * per_group, nz, ny), f32),
            pltpu.VMEM((3, nz, ny), f32),
            pltpu.VMEM((2 * per_group, nz, ny), f32),
            pltpu.VMEM((3, nz, ny), f32),
            pltpu.VMEM((2 * per_group, nz, ny), f32),
        ],
        compiler_params=pltpu.CompilerParams(vmem_limit_bytes=VMEM_LIMIT),
        name="transform",
    )(got_dir, got_maps, got_coils, got_times, got_mask, y_forward, y_backward, z_forward, z_backward)

    packed = (n_kz, COIL_GROUPS + 1, rows, LANES)
    return tuple(pl.pallas_call(
        functools.partial(update_kernel, n_ti, n_kz, per_group),
        out_shape=[
            jax.ShapeDtypeStruct(a.shape, f32)
            for a in (residual_maps, residual_coils, direction_maps, direction_coils)
        ],
        in_specs=[any_, vmem, vmem, vmem, vmem],
        out_specs=[vmem] * 4,
        scratch_shapes=[
            pltpu.VMEM((total, 2, rows, LANES), f32),
            pltpu.VMEM(packed, f32), pltpu.VMEM(packed, f32), pltpu.VMEM(packed, f32),
            pltpu.VMEM((8, LANES), f32), pltpu.VMEM((total, 8, LANES), f32),
            dma((total,)), dma((total,)), dma((total,)), dma((total,)), dma((1,)),
        ],
        compiler_params=pltpu.CompilerParams(
            collective_id=1, has_side_effects=True, vmem_limit_bytes=VMEM_LIMIT
        ),
        name="update",
    )(grads, direction_maps, direction_coils, residual_maps, residual_coils))


def solution(mesh):
    in_specs = (
        P(None, None, "kz", None),
        P(None, None, None, "kz", None),
        P(None, None, "kz", "ti"),
        P(None, None, None, "kz", "ti"),
        P(None, None, "kz", "ti"),
        P(None, None, None, "kz", "ti"),
        P("ti"),
        P("ti", None, None),
    )
    out_specs = (
        P(None, None, "kz", "ti"),
        P(None, None, None, "kz", "ti"),
        P(None, None, "kz", "ti"),
        P(None, None, None, "kz", "ti"),
    )
    body = functools.partial(shards, mesh.shape["ti"], mesh.shape["kz"])
    return jax.shard_map(body, mesh=mesh, in_specs=in_specs, out_specs=out_specs, check_vma=False)
```

```python
import functools
import math

import jax
import jax.numpy as jnp
import ml_dtypes
import numpy as np
from jax import lax
from jax.experimental import pallas as pl
from jax.experimental.pallas import tpu as pltpu
from jax.sharding import PartitionSpec as P

MESH = pl.DeviceIdType.MESH
regular_weight = 2.0
COIL_GROUPS = 4
LANES = 128
VMEM_LIMIT = 48 * 1024 * 1024


def split_table(table):
    high = table.astype(ml_dtypes.bfloat16)
    low = (table - high.astype(np.float64)).astype(ml_dtypes.bfloat16)
    return np.stack([high, low])


def dft_parts(length):
    indices = np.arange(length)
    angles = (indices[:, None] * indices[None, :] % length) * (2.0 * math.pi / length)
    factor = 1.0 / math.sqrt(length)
    return np.cos(angles) * factor, np.sin(angles) * factor


def tables_y(length):
    c, s = dft_parts(length)
    forward = np.block([[c, -s], [s, c]])
    backward = np.block([[c, s], [-s, c]])
    return split_table(forward), split_table(backward)


def tables_z(length):
    c, s = dft_parts(length)
    forward = np.block([[c, s], [-s, c]])
    backward = np.block([[c, -s], [s, c]])
    return split_table(forward), split_table(backward)


def halves(values):
    high = values.astype(jnp.bfloat16)
    low = (values - high.astype(jnp.float32)).astype(jnp.bfloat16)
    return high, low


dot = functools.partial(jnp.dot, preferred_element_type=jnp.float32)


def from_right(values, table):
    high, low = halves(values)
    return dot(high, table[0]) + (dot(low, table[0]) + dot(high, table[1]))


def from_left(table, values):
    high, low = halves(values)
    return dot(table[0], high) + (dot(table[0], low) + dot(table[1], high))


def lane_spans(rows, planes, width):
    count = LANES // (planes * width)
    chunk = -(-(-(-rows // count)) // 8) * 8
    return chunk, [(start, min(chunk, rows - start)) for start in range(0, rows, chunk)]


def lane_blocks(rows, width):
    return lax.broadcasted_iota(jnp.int32, (rows, LANES), 1) // width


def turned(values, shift):
    shift %= LANES
    return pltpu.roll(values, shift, 1) if shift else values


def tall(values, rows):
    missing = rows - values.shape[0]
    if missing:
        values = jnp.concatenate([values, jnp.zeros((missing,) + values.shape[1:], values.dtype)], axis=0)
    return values


def fold(parts, width):
    rows = parts[0].shape[1]
    planes = len(parts)
    chunk, spans = lane_spans(rows, planes, width)
    block = tall(jnp.concatenate(parts, axis=0), LANES).T
    if len(spans) == 1:
        return tall(block, chunk)
    ids = lane_blocks(chunk, planes * width)
    value = jnp.zeros((chunk, LANES), jnp.float32)
    for i, (start, size) in enumerate(spans):
        moved = turned(tall(block[start : start + size], chunk), i * planes * width)
        value = jnp.where(ids == i, moved, value)
    return value


def unfold(block, planes, rows, width):
    _, spans = lane_spans(rows, planes, width)
    parts = [turned(block[:size], -i * planes * width) for i, (_, size) in enumerate(spans)]
    return (jnp.concatenate(parts, axis=0) if len(parts) > 1 else parts[0]).T


def scatter_lanes(blocks, planes, rows, width, store):
    _, spans = lane_spans(rows, planes, width)
    for p in range(planes):
        for i, (start, size) in enumerate(spans):
            ids = lane_blocks(size, width)
            value = None
            for j, block in enumerate(blocks):
                moved = turned(block[:size], (j - i * planes - p) * width)
                value = moved if value is None else jnp.where(ids == j, moved, value)
            store(p, slice(start, start + size), value)


def collect_lanes(planes, j, rows, width):
    chunk, spans = lane_spans(rows, len(planes), width)
    ids = lane_blocks(chunk, width)
    value = jnp.zeros((chunk, LANES), jnp.float32)
    for p, plane in enumerate(planes):
        for i, (start, size) in enumerate(spans):
            q = i * len(planes) + p
            moved = turned(tall(plane[start : start + size], chunk), (q - j) * width)
            value = jnp.where(ids == q, moved, value)
    return value


def step_kernel(
    n_ti, n_kz, per_group, four, one, two,
    dir_maps, dir_coils, res_maps, res_coils, maps, coils, times, mask, tables_y_in, tables_z_in,
    new_res_maps, new_res_coils, new_dir_maps, new_dir_coils,
    send_a, send_b, got_a, got_b, got_maps, got_coils, got_times, got_mask, ytab, ztab,
    p_maps, p_coils, s_maps, s_coils, g_maps, g_coils,
    back_a, back_b, ret_a, ret_b, app_maps, app_coils, sums, got_sums,
    a_out, a_in, b_out, b_in, ra_out, ra_in, rb_out, rb_in, sum_out, sum_in,
    map_out, map_in, coil_out, coil_in, time_out, time_in, mask_out, mask_in, pair_out, pair_in, own,
):
    total = n_ti * n_kz
    ti = lax.axis_index("ti")
    kz = lax.axis_index("kz")
    me = ti * n_kz + kz
    group = lax.rem(ti, COIL_GROUPS)
    first = (ti // COIL_GROUPS) * COIL_GROUPS
    core = lax.rem(kz, 2)
    pair = kz + 1 - 2 * core
    width = dir_maps.shape[2]
    rows = dir_maps.shape[3]
    nz, ny = mask.shape[1:]
    tiles = ny // LANES
    per_tile = LANES // width
    my_coils = pl.ds(group * per_group, per_group)

    barrier = pltpu.get_barrier_semaphore()

    def greet(offset, carry):
        other = lax.rem(me + offset, total)
        pl.semaphore_signal(
            barrier, inc=1, device_id=(other // n_kz, lax.rem(other, n_kz)), device_id_type=MESH
        )
        return carry

    lax.fori_loop(1, total, greet, 0)

    locals_ = [
        pltpu.make_async_copy(maps.at[:, kz], got_maps.at[kz], own.at[0]),
        pltpu.make_async_copy(coils.at[:, my_coils, kz], got_coils.at[kz], own.at[1]),
        pltpu.make_async_copy(times, got_times.at[group], own.at[2]),
        pltpu.make_async_copy(mask, got_mask.at[group], own.at[3]),
        pltpu.make_async_copy(tables_y_in, ytab, own.at[4]),
        pltpu.make_async_copy(tables_z_in, ztab, own.at[5]),
    ]
    for copy in locals_:
        copy.start()

    for x in range(n_kz):
        last = fold([dir_maps[2, x]], width)
        for g in range(COIL_GROUPS):
            c = g * per_group
            send_a[x, g, :four] = fold([dir_coils[0, c, x], dir_coils[1, c, x], dir_maps[0, x], dir_maps[1, x]], width)
            send_a[x, g, four:] = last
            send_b[x, g] = fold([dir_coils[0, c + 1, x], dir_coils[1, c + 1, x]], width)
    got_a[me] = send_a[kz, group]
    got_b[me] = send_b[kz, group]

    pl.semaphore_wait(barrier, total - 1)

    def remote(src, dst, out_sem, in_sem, where):
        return pltpu.make_async_remote_copy(src, dst, out_sem, in_sem, device_id=where, device_id_type=MESH)

    def split_id(other):
        return other // n_kz, lax.rem(other, n_kz)

    def a_copy(other, slot):
        t, k = split_id(other)
        return remote(send_a.at[k, lax.rem(t, COIL_GROUPS)], got_a.at[slot], a_out.at[other], a_in.at[slot], (t, k))

    def b_copy(other, slot):
        t, k = split_id(other)
        return remote(send_b.at[k, lax.rem(t, COIL_GROUPS)], got_b.at[slot], b_out.at[other], b_in.at[slot], (t, k))

    def ra_copy(other, slot):
        return remote(back_a.at[other], ret_a.at[slot], ra_out.at[other], ra_in.at[slot], split_id(other))

    def rb_copy(other, slot):
        return remote(back_b.at[other], ret_b.at[slot], rb_out.at[other], rb_in.at[slot], split_id(other))

    def sum_copy(other, slot):
        return remote(sums, got_sums.at[slot], sum_out.at[other], sum_in.at[slot], split_id(other))

    def send_all(copy):
        def body(offset, carry):
            copy(lax.rem(me + offset, total), me).start()
            return carry

        lax.fori_loop(1, total, body, 0)

    def wait_all(copy):
        def body(offset, carry):
            other = lax.rem(me + offset, total)
            one_copy = copy(other, other)
            one_copy.wait_send()
            one_copy.wait_recv()
            return carry

        lax.fori_loop(1, total, body, 0)

    def point_copies(other, slot):
        return [
            remote(maps.at[:, other], got_maps.at[slot], map_out.at[other], map_in.at[slot], (ti, other)),
            remote(coils.at[:, my_coils, other], got_coils.at[slot], coil_out.at[other], coil_in.at[slot], (ti, other)),
        ]

    def bin_copies(other, slot):
        where = (first + other, kz)
        return [
            remote(times, got_times.at[slot], time_out.at[other], time_in.at[slot], where),
            remote(mask.at[core], got_mask.at[slot, core], mask_out.at[other], mask_in.at[slot], where),
        ]

    def pair_copy(slot, plane):
        where = (ti, pair)
        return remote(got_mask.at[slot, plane], got_mask.at[slot, plane], pair_out.at[slot], pair_in.at[slot], where)

    send_all(a_copy)
    for offset in range(1, n_kz):
        for copy in point_copies(lax.rem(kz + offset, n_kz), kz):
            copy.start()
    for offset in range(1, COIL_GROUPS):
        for copy in bin_copies(lax.rem(group + offset, COIL_GROUPS), group):
            copy.start()
    send_all(b_copy)

    for copy in locals_:
        copy.wait()
    for offset in range(1, n_kz):
        other = lax.rem(kz + offset, n_kz)
        for copy in point_copies(other, other):
            copy.wait_send()
            copy.wait_recv()
    for k in range(n_kz):
        span = slice(k * rows, (k + 1) * rows)
        for m in range(3):
            p_maps[m, span, :] = got_maps[k, m]
        for c in range(per_group):
            for ri in range(2):
                p_coils[2 * c + ri, span, :] = got_coils[k, ri, c]
    wait_all(a_copy)

    def store_to(targets, k, h):
        def store(p, span, value):
            ref, plane = targets[p]
            ref[plane, k * rows + span.start : k * rows + span.stop, h * LANES : (h + 1) * LANES] = value

        return store

    coil_zero = [(s_coils, 0), (s_coils, 1)]
    coil_one = [(s_coils, 2), (s_coils, 3)]
    for k in range(n_kz):
        for h in range(tiles):
            sources = [(h * per_tile + j) * n_kz + k for j in range(per_tile)]
            scatter_lanes(
                [got_a[s, :four] for s in sources], 4, rows, width,
                store_to(coil_zero + [(s_maps, 0), (s_maps, 1)], k, h),
            )
            scatter_lanes([got_a[s, four:] for s in sources], 1, rows, width, store_to([(s_maps, 2)], k, h))

    for offset in range(1, COIL_GROUPS):
        other = lax.rem(group + offset, COIL_GROUPS)
        for copy in bin_copies(other, other):
            copy.wait_send()
            copy.wait_recv()
        pair_copy(other, core).start()

    g_maps[...] = jnp.zeros_like(g_maps)
    g_coils[...] = jnp.zeros_like(g_coils)

    def coil_pass(c):
        def body(offset, carry):
            other = lax.rem(group + offset, COIL_GROUPS)
            if c == 0:
                @pl.when(offset > 0)
                def _():
                    pair_copy(other, core).wait_send()
                    pair_copy(other, 1 - core).wait_recv()

            amplitude = p_maps[1]
            model = []
            rows_in = []
            kept = []
            for b in range(2):
                tau = got_times[other, b, 0:1, 0:1]
                decays = jnp.exp(-tau * p_maps[2])
                signal = p_maps[0] - amplitude * decays
                slope = amplitude * tau * decays
                signal_step = s_maps[0] - s_maps[1] * decays + slope * s_maps[2]
                real = p_coils[2 * c] * signal_step + s_coils[2 * c] * signal
                imag = p_coils[2 * c + 1] * signal_step + s_coils[2 * c + 1] * signal
                rows_in.append(jnp.concatenate([real, imag], axis=1))
                model.append((decays, signal, slope))
                kept.append(got_mask[other, b].astype(jnp.float32))
            both = from_right(jnp.concatenate(rows_in, axis=0), ytab[0])
            along_z = jnp.concatenate(
                [
                    jnp.concatenate([both[b * nz : (b + 1) * nz, :ny], both[b * nz : (b + 1) * nz, ny:]], axis=0)
                    for b in range(2)
                ],
                axis=1,
            )
            kept = jnp.concatenate([jnp.concatenate(kept, axis=1)] * 2, axis=0)
            back = from_left(ztab[1], from_left(ztab[0], along_z) * kept)
            both = jnp.concatenate(
                [
                    jnp.concatenate([back[:nz, b * ny : (b + 1) * ny], back[nz:, b * ny : (b + 1) * ny]], axis=1)
                    for b in range(2)
                ],
                axis=0,
            )
            back = from_right(both, ytab[1])
            for b, (decays, signal, slope) in enumerate(model):
                real = back[b * nz : (b + 1) * nz, :ny]
                imag = back[b * nz : (b + 1) * nz, ny:]
                projected = p_coils[2 * c] * real + p_coils[2 * c + 1] * imag
                g_coils[2 * c] += signal * real
                g_coils[2 * c + 1] += signal * imag
                g_maps[0] += projected
                g_maps[1] -= decays * projected
                g_maps[2] += slope * projected
            return carry

        lax.fori_loop(0, COIL_GROUPS, body, 0)

    coil_pass(0)

    for k in range(n_kz):
        span = slice(k * rows, (k + 1) * rows)
        for h in range(tiles):
            lanes = slice(h * LANES, (h + 1) * LANES)
            planes = [g_coils[p, span, lanes] for p in range(2)]
            for j in range(per_tile):
                back_b[(h * per_tile + j) * n_kz + k] = collect_lanes(planes, j, rows, width)
    send_all(rb_copy)
    ret_b[me] = back_b[me]

    wait_all(b_copy)
    for k in range(n_kz):
        for h in range(tiles):
            sources = [(h * per_tile + j) * n_kz + k for j in range(per_tile)]
            scatter_lanes([got_b[s] for s in sources], 2, rows, width, store_to(coil_one, k, h))

    coil_pass(1)

    for k in range(n_kz):
        span = slice(k * rows, (k + 1) * rows)
        for h in range(tiles):
            lanes = slice(h * LANES, (h + 1) * LANES)
            planes = [g_coils[2, span, lanes], g_coils[3, span, lanes], g_maps[0, span, lanes], g_maps[1, span, lanes]]
            final = [g_maps[2, span, lanes]]
            for j in range(per_tile):
                to = (h * per_tile + j) * n_kz + k
                back_a[to, :four] = collect_lanes(planes, j, rows, width)
                back_a[to, four:] = collect_lanes(final, j, rows, width)
    send_all(ra_copy)
    ret_a[me] = back_a[me]
    wait_all(rb_copy)

    parts = {"old": None, "bend": None, "cross": None, "square": None}

    def settle(applied, grad, d, r):
        a = grad + regular_weight * d
        for key, value in (("old", r * r), ("bend", d * a), ("cross", r * a), ("square", a * a)):
            parts[key] = value if parts[key] is None else parts[key] + value
        return a

    def settle_coils(c, x, flat):
        for ri in range(2):
            grad = flat[ri * width : (ri + 1) * width]
            app_coils[ri, c, x] = settle(None, grad, dir_coils[ri, c, x], res_coils[ri, c, x])

    def added(terms):
        return functools.reduce(lambda u, v: u + v, terms)

    for x in range(n_kz):
        for g in range(COIL_GROUPS):
            block = added([ret_b[t * n_kz + x] for t in range(g, n_ti, COIL_GROUPS)])
            settle_coils(g * per_group, x, unfold(block, 2, rows, width))

    wait_all(ra_copy)
    for x in range(n_kz):
        summed = []
        for g in range(COIL_GROUPS):
            block = added([ret_a[t * n_kz + x, :four] for t in range(g, n_ti, COIL_GROUPS)])
            summed.append(block)
            settle_coils(g * per_group + 1, x, unfold(block, 4, rows, width))
        flat = unfold(added(summed), 4, rows, width)
        final = unfold(added([ret_a[t * n_kz + x, four:] for t in range(n_ti)]), 1, rows, width)
        grads = [flat[2 * width : 3 * width], flat[3 * width : 4 * width], final[:width]]
        for m, grad in enumerate(grads):
            app_maps[m, x] = settle(None, grad, dir_maps[m, x], res_maps[m, x])

    row = lax.broadcasted_iota(jnp.int32, sums.shape, 0)
    tile = jnp.zeros(sums.shape, jnp.float32)
    for i, part in enumerate(parts.values()):
        tile = jnp.where(row == i, jnp.sum(part, keepdims=True), tile)
    sums[...] = tile
    send_all(sum_copy)
    got_sums[me] = tile
    wait_all(sum_copy)
    whole = jnp.sum(got_sums[...], axis=0)
    old, bend, cross, square = (whole[i : i + 1, :rows] for i in range(4))
    step = old / bend
    ratio = (old - 2.0 * step * cross + step * step * square) / old
    for x in range(n_kz):
        for m in range(3):
            r = res_maps[m, x] - step * app_maps[m, x]
            new_res_maps[m, x] = r
            new_dir_maps[m, x] = r + ratio * dir_maps[m, x]
        for c in range(COIL_GROUPS * per_group):
            for ri in range(2):
                r = res_coils[ri, c, x] - step * app_coils[ri, c, x]
                new_res_coils[ri, c, x] = r
                new_dir_coils[ri, c, x] = r + ratio * dir_coils[ri, c, x]


def shards(
    n_ti, n_kz,
    point_maps, point_coils, direction_maps, direction_coils,
    residual_maps, residual_coils, inversion_times, sampling_mask,
):
    total = n_ti * n_kz
    coils = point_coils.shape[1]
    per_group = coils // COIL_GROUPS
    rows, ny = point_maps.shape[2:]
    width = ny // n_ti
    local_bins, nz, _ = sampling_mask.shape
    f32 = jnp.float32
    any_ = pl.BlockSpec(memory_space=pl.ANY)
    vmem = pl.BlockSpec(memory_space=pltpu.VMEM)
    dma = pltpu.SemaphoreType.DMA
    times = jnp.broadcast_to(inversion_times[:, None, None], (local_bins, 8, LANES))
    y_tables = jnp.asarray(np.stack(tables_y(ny)))
    z_tables = jnp.asarray(np.stack(tables_z(nz)))
    flipped = [
        jnp.swapaxes(a, -1, -2) for a in (direction_maps, direction_coils, residual_maps, residual_coils)
    ]
    four, one, two = (lane_spans(rows, planes, width)[0] for planes in (4, 1, 2))
    a_rows = four + one

    outs = pl.pallas_call(
        functools.partial(step_kernel, n_ti, n_kz, per_group, four, one, two),
        out_shape=[jax.ShapeDtypeStruct(flipped[i].shape, f32) for i in (2, 3, 0, 1)],
        in_specs=[vmem] * 4 + [any_] * 6,
        out_specs=[vmem] * 4,
        scratch_shapes=[
            pltpu.VMEM((n_kz, COIL_GROUPS, a_rows, LANES), f32),
            pltpu.VMEM((n_kz, COIL_GROUPS, two, LANES), f32),
            pltpu.VMEM((total, a_rows, LANES), f32),
            pltpu.VMEM((total, two, LANES), f32),
            pltpu.VMEM((n_kz, 3, rows, ny), f32),
            pltpu.VMEM((n_kz, 2, per_group, rows, ny), f32),
            pltpu.VMEM((COIL_GROUPS,) + times.shape, f32),
            pltpu.VMEM((COIL_GROUPS,) + sampling_mask.shape, jnp.int32),
            pltpu.VMEM(y_tables.shape, jnp.bfloat16),
            pltpu.VMEM(z_tables.shape, jnp.bfloat16),
            pltpu.VMEM((3, nz, ny), f32),
            pltpu.VMEM((2 * per_group, nz, ny), f32),
            pltpu.VMEM((3, nz, ny), f32),
            pltpu.VMEM((2 * per_group, nz, ny), f32),
            pltpu.VMEM((3, nz, ny), f32),
            pltpu.VMEM((2 * per_group, nz, ny), f32),
            pltpu.VMEM((total, a_rows, LANES), f32),
            pltpu.VMEM((total, two, LANES), f32),
            pltpu.VMEM((total, a_rows, LANES), f32),
            pltpu.VMEM((total, two, LANES), f32),
            pltpu.VMEM(flipped[0].shape, f32),
            pltpu.VMEM(flipped[1].shape, f32),
            pltpu.VMEM((8, LANES), f32),
            pltpu.VMEM((total, 8, LANES), f32),
        ]
        + [dma((total,))] * 10
        + [dma((n_kz,))] * 4
        + [dma((COIL_GROUPS,))] * 6
        + [dma((6,))],
        compiler_params=pltpu.CompilerParams(
            collective_id=0, has_side_effects=True, vmem_limit_bytes=VMEM_LIMIT
        ),
        name="step",
    )(*flipped, point_maps, point_coils, times, sampling_mask, y_tables, z_tables)
    return tuple(jnp.swapaxes(a, -1, -2) for a in outs)


def solution(mesh):
    in_specs = (
        P(None, None, "kz", None),
        P(None, None, None, "kz", None),
        P(None, None, "kz", "ti"),
        P(None, None, None, "kz", "ti"),
        P(None, None, "kz", "ti"),
        P(None, None, None, "kz", "ti"),
        P("ti"),
        P("ti", None, None),
    )
    out_specs = (
        P(None, None, "kz", "ti"),
        P(None, None, None, "kz", "ti"),
        P(None, None, "kz", "ti"),
        P(None, None, None, "kz", "ti"),
    )
    body = functools.partial(shards, mesh.shape["ti"], mesh.shape["kz"])
    return jax.shard_map(body, mesh=mesh, in_specs=in_specs, out_specs=out_specs, check_vma=False)
```

```python
import functools
import math

import jax
import jax.numpy as jnp
import numpy as np
from jax import lax
from jax.experimental import pallas as pl
from jax.experimental.pallas import tpu as pltpu
from jax.sharding import PartitionSpec as P

MESH = pl.DeviceIdType.MESH
regular_weight = 2.0
COIL_GROUPS = 4
LANES = 128
VMEM_LIMIT = 60 * 1024 * 1024


def half_parts(length, parity):
    points = np.arange(length // 2)
    orders = 2 * points + parity
    angles = (points[:, None] * orders[None, :] % length) * (2.0 * math.pi / length)
    factor = 1.0 / math.sqrt(length)
    return np.cos(angles) * factor, np.sin(angles) * factor


def tables_y(length):
    forward, backward = [], []
    for parity in range(2):
        c, s = half_parts(length, parity)
        forward.append(np.block([[c, -s], [s, c]]))
        backward.append(np.block([[c.T, s.T], [-s.T, c.T]]))
    return np.stack([np.stack(forward), np.stack(backward)]).astype(np.float32)


def tables_z(length):
    forward, backward = [], []
    for parity in range(2):
        c, s = half_parts(length, parity)
        forward.append(np.block([[c.T, s.T], [-s.T, c.T]]))
        backward.append(np.block([[c, -s], [s, c]]))
    return np.stack([np.stack(forward), np.stack(backward)]).astype(np.float32)


def even_then_odd(length, source_axis):
    source = lax.broadcasted_iota(jnp.int32, (length, length), source_axis)
    place = lax.broadcasted_iota(jnp.int32, (length, length), 1 - source_axis)
    wanted = jnp.where(place < length // 2, 2 * place, 2 * place - length + 1)
    return jnp.where(source == wanted, 1.0, 0.0).astype(jnp.bfloat16)


def halves(values):
    high = values.astype(jnp.bfloat16)
    low = (values - high.astype(jnp.float32)).astype(jnp.bfloat16)
    return high, low


dot = functools.partial(jnp.dot, preferred_element_type=jnp.float32)


def from_right(values, table):
    high, low = halves(values)
    return dot(high, table[0]) + (dot(low, table[0]) + dot(high, table[1]))


def from_left(table, values):
    high, low = halves(values)
    size = table.shape[1]
    both = dot(table, high)
    return both[:size] + (both[size:] + dot(table[:size], low))


def lane_spans(rows, planes, width):
    count = LANES // (planes * width)
    chunk = -(-(-(-rows // count)) // 8) * 8
    return chunk, [(start, min(chunk, rows - start)) for start in range(0, rows, chunk)]


def lane_blocks(rows, width):
    return lax.broadcasted_iota(jnp.int32, (rows, LANES), 1) // width


def turned(values, shift):
    shift %= LANES
    return pltpu.roll(values, shift, 1) if shift else values


def tall(values, rows):
    missing = rows - values.shape[0]
    if missing:
        values = jnp.concatenate([values, jnp.zeros((missing,) + values.shape[1:], values.dtype)], axis=0)
    return values


def fold(parts, width):
    rows = parts[0].shape[1]
    planes = len(parts)
    chunk, spans = lane_spans(rows, planes, width)
    block = tall(jnp.concatenate(parts, axis=0), LANES).T
    if len(spans) == 1:
        return tall(block, chunk)
    ids = lane_blocks(chunk, planes * width)
    value = jnp.zeros((chunk, LANES), jnp.float32)
    for i, (start, size) in enumerate(spans):
        moved = turned(tall(block[start : start + size], chunk), i * planes * width)
        value = jnp.where(ids == i, moved, value)
    return value


def unfold(block, planes, rows, width):
    _, spans = lane_spans(rows, planes, width)
    parts = [turned(block[:size], -i * planes * width) for i, (_, size) in enumerate(spans)]
    return (jnp.concatenate(parts, axis=0) if len(parts) > 1 else parts[0]).T


def scatter_lanes(blocks, planes, rows, width, store):
    _, spans = lane_spans(rows, planes, width)
    for p in range(planes):
        for i, (start, size) in enumerate(spans):
            ids = lane_blocks(size, width)
            value = None
            for j, block in enumerate(blocks):
                moved = turned(block[:size], (j - i * planes - p) * width)
                value = moved if value is None else jnp.where(ids == j, moved, value)
            store(p, slice(start, start + size), value)


def collect_lanes(planes, j, rows, width):
    chunk, spans = lane_spans(rows, len(planes), width)
    ids = lane_blocks(chunk, width)
    value = jnp.zeros((chunk, LANES), jnp.float32)
    for p, plane in enumerate(planes):
        for i, (start, size) in enumerate(spans):
            q = i * len(planes) + p
            moved = turned(tall(plane[start : start + size], chunk), (q - j) * width)
            value = jnp.where(ids == q, moved, value)
    return value


def step_kernel(
    n_ti, n_kz, per_group, four, one, two,
    dir_maps_in, dir_coils_in, res_maps_in, res_coils_in, maps, coils, bin_times, mask,
    tables_y_in, tables_z_in,
    app_maps, app_coils, scales,
    dir_maps, dir_coils, res_maps, res_coils, times, order_y, order_z, kept_masks, wide_y, wide_z,
    send_a, send_b, got_a, got_b, got_maps, got_coils, got_times, got_mask, ytab, ztab,
    p_maps, p_coils, s_maps, s_coils, g_maps, g_coils,
    back_a, back_b, ret_a, ret_b, sums, got_sums,
    a_out, a_in, b_out, b_in, ra_out, ra_in, rb_out, rb_in, sum_out, sum_in,
    map_out, map_in, coil_out, coil_in, time_out, time_in, mask_out, mask_in, pair_out, pair_in, own,
):
    total = n_ti * n_kz
    ti = lax.axis_index("ti")
    kz = lax.axis_index("kz")
    me = ti * n_kz + kz
    group = lax.rem(ti, COIL_GROUPS)
    first = (ti // COIL_GROUPS) * COIL_GROUPS
    core = lax.rem(kz, 2)
    pair = kz + 1 - 2 * core
    width = dir_maps.shape[2]
    rows = dir_maps.shape[3]
    nz, ny = mask.shape[1:]
    tiles = ny // LANES
    per_tile = LANES // width
    my_coils = pl.ds(group * per_group, per_group)

    early = [
        pltpu.make_async_copy(dir_maps_in, dir_maps, own.at[6]),
        pltpu.make_async_copy(dir_coils_in, dir_coils, own.at[7]),
    ]
    for copy in early:
        copy.start()

    barrier = pltpu.get_barrier_semaphore()

    def greet(offset, carry):
        other = lax.rem(me + offset, total)
        pl.semaphore_signal(
            barrier, inc=1, device_id=(other // n_kz, lax.rem(other, n_kz)), device_id_type=MESH
        )
        return carry

    lax.fori_loop(1, total, greet, 0)

    locals_ = [
        pltpu.make_async_copy(maps.at[:, kz], got_maps.at[kz], own.at[0]),
        pltpu.make_async_copy(coils.at[:, my_coils, kz], got_coils.at[kz], own.at[1]),
        pltpu.make_async_copy(mask, got_mask.at[group], own.at[3]),
        pltpu.make_async_copy(tables_y_in, wide_y, own.at[4]),
        pltpu.make_async_copy(tables_z_in, wide_z, own.at[5]),
        pltpu.make_async_copy(res_maps_in, res_maps, own.at[2]),
        pltpu.make_async_copy(res_coils_in, res_coils, own.at[8]),
    ]
    for copy in locals_:
        copy.start()
    for b in range(2):
        times[b] = jnp.full((8, LANES), bin_times[b], jnp.float32)
        got_times[group, b] = jnp.full((8, LANES), bin_times[b], jnp.float32)
    for copy in early:
        copy.wait()

    for x in range(n_kz):
        last = fold([dir_maps[2, x]], width)
        for g in range(COIL_GROUPS):
            c = g * per_group
            send_a[x, g, :four] = fold([dir_coils[0, c, x], dir_coils[1, c, x], dir_maps[0, x], dir_maps[1, x]], width)
            send_a[x, g, four:] = last
            send_b[x, g] = fold([dir_coils[0, c + 1, x], dir_coils[1, c + 1, x]], width)
    got_a[me] = send_a[kz, group]
    got_b[me] = send_b[kz, group]

    pl.semaphore_wait(barrier, total - 1)

    def remote(src, dst, out_sem, in_sem, where):
        return pltpu.make_async_remote_copy(src, dst, out_sem, in_sem, device_id=where, device_id_type=MESH)

    def split_id(other):
        return other // n_kz, lax.rem(other, n_kz)

    def a_copy(other, slot):
        t, k = split_id(other)
        return remote(send_a.at[k, lax.rem(t, COIL_GROUPS)], got_a.at[slot], a_out.at[other], a_in.at[slot], (t, k))

    def b_copy(other, slot):
        t, k = split_id(other)
        return remote(send_b.at[k, lax.rem(t, COIL_GROUPS)], got_b.at[slot], b_out.at[other], b_in.at[slot], (t, k))

    def ra_copy(other, slot):
        return remote(back_a.at[other], ret_a.at[slot], ra_out.at[other], ra_in.at[slot], split_id(other))

    def rb_copy(other, slot):
        return remote(back_b.at[other], ret_b.at[slot], rb_out.at[other], rb_in.at[slot], split_id(other))

    def sum_copy(other, slot):
        return remote(sums, got_sums.at[slot], sum_out.at[other], sum_in.at[slot], split_id(other))

    def send_all(copy):
        def body(offset, carry):
            copy(lax.rem(me + offset, total), me).start()
            return carry

        lax.fori_loop(1, total, body, 0)

    def wait_all(copy):
        def body(offset, carry):
            other = lax.rem(me + offset, total)
            one_copy = copy(other, other)
            one_copy.wait_send()
            one_copy.wait_recv()
            return carry

        lax.fori_loop(1, total, body, 0)

    def point_copies(other, slot):
        return [
            remote(maps.at[:, other], got_maps.at[slot], map_out.at[other], map_in.at[slot], (ti, other)),
            remote(coils.at[:, my_coils, other], got_coils.at[slot], coil_out.at[other], coil_in.at[slot], (ti, other)),
        ]

    def bin_copies(other, slot):
        where = (first + other, kz)
        return [
            remote(times, got_times.at[slot], time_out.at[other], time_in.at[slot], where),
            remote(mask.at[core], got_mask.at[slot, core], mask_out.at[other], mask_in.at[slot], where),
        ]

    def pair_copy(slot, plane):
        where = (ti, pair)
        return remote(got_mask.at[slot, plane], got_mask.at[slot, plane], pair_out.at[slot], pair_in.at[slot], where)

    send_all(a_copy)
    for offset in range(1, n_kz):
        for copy in point_copies(lax.rem(kz + offset, n_kz), kz):
            copy.start()
    for offset in range(1, COIL_GROUPS):
        for copy in bin_copies(lax.rem(group + offset, COIL_GROUPS), group):
            copy.start()
    send_all(b_copy)

    for copy in locals_:
        copy.wait()
    order_y[...] = even_then_odd(ny, 0)
    order_z[...] = even_then_odd(nz, 1)
    for way in range(2):
        for parity in range(2):
            high, low = halves(wide_y[way, parity])
            ytab[way, parity, 0] = high
            ytab[way, parity, 1] = low
            high, low = halves(wide_z[way, parity])
            ztab[way, parity, :nz] = high
            ztab[way, parity, nz:] = low
    for offset in range(1, n_kz):
        other = lax.rem(kz + offset, n_kz)
        for copy in point_copies(other, other):
            copy.wait_send()
            copy.wait_recv()
    for k in range(n_kz):
        span = slice(k * rows, (k + 1) * rows)
        for m in range(3):
            p_maps[m, span, :] = got_maps[k, m]
        for c in range(per_group):
            for ri in range(2):
                p_coils[2 * c + ri, span, :] = got_coils[k, ri, c]
    wait_all(a_copy)

    def store_to(targets, k, h):
        def store(p, span, value):
            ref, plane = targets[p]
            ref[plane, k * rows + span.start : k * rows + span.stop, h * LANES : (h + 1) * LANES] = value

        return store

    coil_zero = [(s_coils, 0), (s_coils, 1)]
    coil_one = [(s_coils, 2), (s_coils, 3)]
    for k in range(n_kz):
        for h in range(tiles):
            sources = [(h * per_tile + j) * n_kz + k for j in range(per_tile)]
            scatter_lanes(
                [got_a[s, :four] for s in sources], 4, rows, width,
                store_to(coil_zero + [(s_maps, 0), (s_maps, 1)], k, h),
            )
            scatter_lanes([got_a[s, four:] for s in sources], 1, rows, width, store_to([(s_maps, 2)], k, h))

    g_maps[...] = jnp.zeros_like(g_maps)
    g_coils[...] = jnp.zeros_like(g_coils)

    def coil_pass(c):
        def body(offset, carry):
            other = lax.rem(group + offset, COIL_GROUPS)
            if c == 0:
                if not isinstance(offset, int):
                    pair_copy(other, core).wait_send()
                    pair_copy(other, 1 - core).wait_recv()
                bits = jnp.concatenate([got_mask[other, 0], got_mask[other, 1]], axis=0)
                bits = dot(bits.astype(jnp.float32).astype(jnp.bfloat16), order_y[...])
                bits = jnp.concatenate([bits[:nz], bits[nz:]], axis=1).astype(jnp.bfloat16)
                kept_masks[other] = dot(order_z[...], bits)

            amplitude = p_maps[1]
            model = []
            rows_in = []
            for b in range(2):
                tau = got_times[other, b, 0:1, 0:1]
                decays = jnp.exp(-tau * p_maps[2])
                signal = p_maps[0] - amplitude * decays
                slope = amplitude * tau * decays
                signal_step = s_maps[0] - s_maps[1] * decays + slope * s_maps[2]
                real = p_coils[2 * c] * signal_step + s_coils[2 * c] * signal
                imag = p_coils[2 * c + 1] * signal_step + s_coils[2 * c + 1] * signal
                rows_in.append(jnp.concatenate([real, imag], axis=1))
                model.append((decays, signal, slope))
            x = jnp.concatenate(rows_in, axis=0)
            h = ny // 2
            left, right = [jnp.concatenate([x[:, o : o + h], x[:, ny + o : ny + o + h]], axis=1) for o in (0, h)]
            even = from_right(left + right, ytab[0, 0])
            odd = from_right(left - right, ytab[0, 1])
            parts_z = []
            for o in (0, h):
                parts_z.append(
                    jnp.concatenate(
                        [
                            v
                            for b in range(2)
                            for v in (even[b * nz : (b + 1) * nz, o : o + h], odd[b * nz : (b + 1) * nz, o : o + h])
                        ],
                        axis=1,
                    )
                )
            q = nz // 2
            top = jnp.concatenate([v[:q] for v in parts_z], axis=0)
            bottom = jnp.concatenate([v[q:] for v in parts_z], axis=0)
            kept_even = kept_masks[other, :q]
            kept_odd = kept_masks[other, q:]
            even = from_left(ztab[0, 0], top + bottom) * jnp.concatenate([kept_even] * 2, axis=0)
            odd = from_left(ztab[0, 1], top - bottom) * jnp.concatenate([kept_odd] * 2, axis=0)
            even = from_left(ztab[1, 0], even)
            odd = from_left(ztab[1, 1], odd)
            top, bottom = even + odd, even - odd
            real = jnp.concatenate([top[:q], bottom[:q]], axis=0)
            imag = jnp.concatenate([top[q:], bottom[q:]], axis=0)
            even, odd = [
                jnp.concatenate(
                    [
                        jnp.concatenate([v[:, b * ny + o : b * ny + o + h] for v in (real, imag)], axis=1)
                        for b in range(2)
                    ],
                    axis=0,
                )
                for o in (0, h)
            ]
            even = from_right(even, ytab[1, 0])
            odd = from_right(odd, ytab[1, 1])
            left, right = even + odd, even - odd
            for b, (decays, signal, slope) in enumerate(model):
                span = slice(b * nz, (b + 1) * nz)
                real = jnp.concatenate([left[span, :h], right[span, :h]], axis=1)
                imag = jnp.concatenate([left[span, h:], right[span, h:]], axis=1)
                projected = p_coils[2 * c] * real + p_coils[2 * c + 1] * imag
                g_coils[2 * c] += signal * real
                g_coils[2 * c + 1] += signal * imag
                g_maps[0] += projected
                g_maps[1] -= decays * projected
                g_maps[2] += slope * projected
            return carry

        if c == 0:
            body(0, 0)
            for offset in range(1, COIL_GROUPS):
                other = lax.rem(group + offset, COIL_GROUPS)
                for copy in bin_copies(other, other):
                    copy.wait_send()
                    copy.wait_recv()
                pair_copy(other, core).start()
            lax.fori_loop(1, COIL_GROUPS, body, 0)
        else:
            lax.fori_loop(0, COIL_GROUPS, body, 0)

    coil_pass(0)

    for k in range(n_kz):
        span = slice(k * rows, (k + 1) * rows)
        for h in range(tiles):
            lanes = slice(h * LANES, (h + 1) * LANES)
            planes = [g_coils[p, span, lanes] for p in range(2)]
            for j in range(per_tile):
                back_b[(h * per_tile + j) * n_kz + k] = collect_lanes(planes, j, rows, width)
    send_all(rb_copy)
    ret_b[me] = back_b[me]

    wait_all(b_copy)
    for k in range(n_kz):
        for h in range(tiles):
            sources = [(h * per_tile + j) * n_kz + k for j in range(per_tile)]
            scatter_lanes([got_b[s] for s in sources], 2, rows, width, store_to(coil_one, k, h))

    coil_pass(1)

    for k in range(n_kz):
        span = slice(k * rows, (k + 1) * rows)
        for h in range(tiles):
            lanes = slice(h * LANES, (h + 1) * LANES)
            planes = [g_coils[2, span, lanes], g_coils[3, span, lanes], g_maps[0, span, lanes], g_maps[1, span, lanes]]
            final = [g_maps[2, span, lanes]]
            for j in range(per_tile):
                to = (h * per_tile + j) * n_kz + k
                back_a[to, :four] = collect_lanes(planes, j, rows, width)
                back_a[to, four:] = collect_lanes(final, j, rows, width)
    send_all(ra_copy)
    ret_a[me] = back_a[me]
    wait_all(rb_copy)

    parts = {"old": None, "bend": None, "cross": None, "square": None}

    def settle(applied, grad, d, r):
        a = grad + regular_weight * d
        for key, value in (("old", r * r), ("bend", d * a), ("cross", r * a), ("square", a * a)):
            parts[key] = value if parts[key] is None else parts[key] + value
        return a

    def settle_coils(c, x, flat):
        for ri in range(2):
            grad = flat[ri * width : (ri + 1) * width]
            app_coils[ri, c, x] = settle(None, grad, dir_coils[ri, c, x], res_coils[ri, c, x])

    def added(terms):
        return functools.reduce(lambda u, v: u + v, terms)

    for x in range(n_kz):
        for g in range(COIL_GROUPS):
            block = added([ret_b[t * n_kz + x] for t in range(g, n_ti, COIL_GROUPS)])
            settle_coils(g * per_group, x, unfold(block, 2, rows, width))

    wait_all(ra_copy)
    for x in range(n_kz):
        summed = []
        for g in range(COIL_GROUPS):
            block = added([ret_a[t * n_kz + x, :four] for t in range(g, n_ti, COIL_GROUPS)])
            summed.append(block)
            settle_coils(g * per_group + 1, x, unfold(block, 4, rows, width))
        flat = unfold(added(summed), 4, rows, width)
        final = unfold(added([ret_a[t * n_kz + x, four:] for t in range(n_ti)]), 1, rows, width)
        grads = [flat[2 * width : 3 * width], flat[3 * width : 4 * width], final[:width]]
        for m, grad in enumerate(grads):
            app_maps[m, x] = settle(None, grad, dir_maps[m, x], res_maps[m, x])

    row = lax.broadcasted_iota(jnp.int32, sums.shape, 0)
    tile = jnp.zeros(sums.shape, jnp.float32)
    for i, part in enumerate(parts.values()):
        tile = jnp.where(row == i, jnp.sum(part, keepdims=True), tile)
    sums[...] = tile
    send_all(sum_copy)
    got_sums[me] = tile
    wait_all(sum_copy)
    whole = jnp.sum(got_sums[...], axis=0)
    old, bend, cross, square = (whole[i : i + 1, :] for i in range(4))
    step = old / bend
    ratio = (old - 2.0 * step * cross + step * step * square) / old
    scales[0] = jnp.broadcast_to(step, scales.shape[1:])
    scales[1] = jnp.broadcast_to(ratio, scales.shape[1:])


def shards(
    n_ti, n_kz,
    point_maps, point_coils, direction_maps, direction_coils,
    residual_maps, residual_coils, inversion_times, sampling_mask,
):
    total = n_ti * n_kz
    coils = point_coils.shape[1]
    per_group = coils // COIL_GROUPS
    rows, ny = point_maps.shape[2:]
    width = ny // n_ti
    local_bins, nz, _ = sampling_mask.shape
    f32 = jnp.float32
    vmem = pl.BlockSpec(memory_space=pltpu.VMEM)
    dma = pltpu.SemaphoreType.DMA
    hbm = pl.BlockSpec(memory_space=pltpu.HBM)
    tables = [jnp.asarray(t) for t in (tables_y(ny), tables_z(nz))]
    flipped = [
        jnp.swapaxes(a, -1, -2) for a in (direction_maps, direction_coils, residual_maps, residual_coils)
    ]
    four, one, two = (lane_spans(rows, planes, width)[0] for planes in (4, 1, 2))
    a_rows = four + one

    outs = pl.pallas_call(
        functools.partial(step_kernel, n_ti, n_kz, per_group, four, one, two),
        out_shape=[jax.ShapeDtypeStruct(shape, f32) for shape in (flipped[0].shape, flipped[1].shape, (2, 8, LANES))],
        in_specs=[hbm] * 6 + [pl.BlockSpec(memory_space=pltpu.SMEM)] + [hbm] * 3,
        out_specs=[vmem] * 3,
        scratch_shapes=[
            *(pltpu.VMEM(a.shape, f32) for a in flipped),
            pltpu.VMEM((local_bins, 8, LANES), f32),
            pltpu.VMEM((ny, ny), jnp.bfloat16),
            pltpu.VMEM((nz, nz), jnp.bfloat16),
            pltpu.VMEM((COIL_GROUPS, nz, 2 * ny), f32),
            *(pltpu.VMEM(t.shape, f32) for t in tables),
            pltpu.VMEM((n_kz, COIL_GROUPS, a_rows, LANES), f32),
            pltpu.VMEM((n_kz, COIL_GROUPS, two, LANES), f32),
            pltpu.VMEM((total, a_rows, LANES), f32),
            pltpu.VMEM((total, two, LANES), f32),
            pltpu.VMEM((n_kz, 3, rows, ny), f32),
            pltpu.VMEM((n_kz, 2, per_group, rows, ny), f32),
            pltpu.VMEM((COIL_GROUPS, local_bins, 8, LANES), f32),
            pltpu.VMEM((COIL_GROUPS,) + sampling_mask.shape, jnp.int32),
            pltpu.VMEM((2, 2, 2, ny, ny), jnp.bfloat16),
            pltpu.VMEM((2, 2, 2 * nz, nz), jnp.bfloat16),
            pltpu.VMEM((3, nz, ny), f32),
            pltpu.VMEM((2 * per_group, nz, ny), f32),
            pltpu.VMEM((3, nz, ny), f32),
            pltpu.VMEM((2 * per_group, nz, ny), f32),
            pltpu.VMEM((3, nz, ny), f32),
            pltpu.VMEM((2 * per_group, nz, ny), f32),
            pltpu.VMEM((total, a_rows, LANES), f32),
            pltpu.VMEM((total, two, LANES), f32),
            pltpu.VMEM((total, a_rows, LANES), f32),
            pltpu.VMEM((total, two, LANES), f32),
            pltpu.VMEM((8, LANES), f32),
            pltpu.VMEM((total, 8, LANES), f32),
        ]
        + [dma((total,))] * 10
        + [dma((n_kz,))] * 4
        + [dma((COIL_GROUPS,))] * 6
        + [dma((9,))],
        compiler_params=pltpu.CompilerParams(
            collective_id=0, has_side_effects=True, vmem_limit_bytes=VMEM_LIMIT
        ),
        name="step",
    )(*flipped, point_maps, point_coils, inversion_times, sampling_mask, *tables)
    applied = [jnp.swapaxes(a, -1, -2) for a in outs[:2]]
    step, ratio = outs[2][0, 0, 0], outs[2][1, 0, 0]
    new_residual = [r - step * a for r, a in zip((residual_maps, residual_coils), applied)]
    new_direction = [r + ratio * d for r, d in zip(new_residual, (direction_maps, direction_coils))]
    return (*new_residual, *new_direction)


def solution(mesh):
    in_specs = (
        P(None, None, "kz", None),
        P(None, None, None, "kz", None),
        P(None, None, "kz", "ti"),
        P(None, None, None, "kz", "ti"),
        P(None, None, "kz", "ti"),
        P(None, None, None, "kz", "ti"),
        P("ti"),
        P("ti", None, None),
    )
    out_specs = (
        P(None, None, "kz", "ti"),
        P(None, None, None, "kz", "ti"),
        P(None, None, "kz", "ti"),
        P(None, None, None, "kz", "ti"),
    )
    body = functools.partial(shards, mesh.shape["ti"], mesh.shape["kz"])
    return jax.shard_map(body, mesh=mesh, in_specs=in_specs, out_specs=out_specs, check_vma=False)
```

```python
import functools
import math

import jax
import jax.numpy as jnp
import numpy as np
from jax import lax
from jax.experimental import pallas as pl
from jax.experimental.pallas import tpu as pltpu
from jax.sharding import PartitionSpec as P

MESH = pl.DeviceIdType.MESH
regular_weight = 2.0
COIL_GROUPS = 4
LANES = 128
VMEM_LIMIT = 60 * 1024 * 1024


def half_parts(length, parity):
    points = np.arange(length // 2)
    orders = 2 * points + parity
    angles = (points[:, None] * orders[None, :] % length) * (2.0 * math.pi / length)
    factor = 1.0 / math.sqrt(length)
    return np.cos(angles) * factor, np.sin(angles) * factor


def tables_y(length):
    forward, backward = [], []
    for parity in range(2):
        c, s = half_parts(length, parity)
        forward.append(np.block([[c, -s], [s, c]]))
        backward.append(np.block([[c.T, s.T], [-s.T, c.T]]))
    return np.stack([np.stack(forward), np.stack(backward)]).astype(np.float32)


def tables_z(length):
    forward, backward = [], []
    for parity in range(2):
        c, s = half_parts(length, parity)
        forward.append(np.block([[c.T, s.T], [-s.T, c.T]]))
        backward.append(np.block([[c, -s], [s, c]]))
    return np.stack([np.stack(forward), np.stack(backward)]).astype(np.float32)


def even_then_odd(length, source_axis):
    source = lax.broadcasted_iota(jnp.int32, (length, length), source_axis)
    place = lax.broadcasted_iota(jnp.int32, (length, length), 1 - source_axis)
    wanted = jnp.where(place < length // 2, 2 * place, 2 * place - length + 1)
    return jnp.where(source == wanted, 1.0, 0.0).astype(jnp.bfloat16)


def halves(values):
    high = values.astype(jnp.bfloat16)
    low = (values - high.astype(jnp.float32)).astype(jnp.bfloat16)
    return high, low


dot = functools.partial(jnp.dot, preferred_element_type=jnp.float32)


def from_right(values, table):
    high, low = halves(values)
    return dot(high, table[0]) + (dot(low, table[0]) + dot(high, table[1]))


def from_left(table, values):
    high, low = halves(values)
    size = table.shape[1]
    both = dot(table, high)
    return both[:size] + (both[size:] + dot(table[:size], low))


def lane_spans(rows, planes, width):
    count = LANES // (planes * width)
    chunk = -(-(-(-rows // count)) // 8) * 8
    return chunk, [(start, min(chunk, rows - start)) for start in range(0, rows, chunk)]


def lane_blocks(rows, width):
    return lax.broadcasted_iota(jnp.int32, (rows, LANES), 1) // width


def turned(values, shift):
    shift %= LANES
    return pltpu.roll(values, shift, 1) if shift else values


def tall(values, rows):
    missing = rows - values.shape[0]
    if missing:
        values = jnp.concatenate([values, jnp.zeros((missing,) + values.shape[1:], values.dtype)], axis=0)
    return values


def fold(parts, width):
    rows = parts[0].shape[1]
    planes = len(parts)
    chunk, spans = lane_spans(rows, planes, width)
    block = tall(jnp.concatenate(parts, axis=0), LANES).T
    if len(spans) == 1:
        return tall(block, chunk)
    ids = lane_blocks(chunk, planes * width)
    value = jnp.zeros((chunk, LANES), jnp.float32)
    for i, (start, size) in enumerate(spans):
        moved = turned(tall(block[start : start + size], chunk), i * planes * width)
        value = jnp.where(ids == i, moved, value)
    return value


def unfold(block, planes, rows, width):
    _, spans = lane_spans(rows, planes, width)
    parts = [turned(block[:size], -i * planes * width) for i, (_, size) in enumerate(spans)]
    return (jnp.concatenate(parts, axis=0) if len(parts) > 1 else parts[0]).T


def scatter_lanes(blocks, planes, rows, width, store):
    _, spans = lane_spans(rows, planes, width)
    for p in range(planes):
        for i, (start, size) in enumerate(spans):
            ids = lane_blocks(size, width)
            value = None
            for j, block in enumerate(blocks):
                moved = turned(block[:size], (j - i * planes - p) * width)
                value = moved if value is None else jnp.where(ids == j, moved, value)
            store(p, slice(start, start + size), value)


def collect_lanes(planes, j, rows, width):
    chunk, spans = lane_spans(rows, len(planes), width)
    ids = lane_blocks(chunk, width)
    value = jnp.zeros((chunk, LANES), jnp.float32)
    for p, plane in enumerate(planes):
        for i, (start, size) in enumerate(spans):
            q = i * len(planes) + p
            moved = turned(tall(plane[start : start + size], chunk), (q - j) * width)
            value = jnp.where(ids == q, moved, value)
    return value


def step_kernel(
    n_ti, n_kz, per_group,
    dir_maps_in, dir_coils_in, res_maps_in, res_coils_in, maps, coils, bin_times, mask,
    tables_y_in, tables_z_in,
    app_maps, app_coils, scales,
    dir_maps, dir_coils, res_maps, res_coils, times, order_y, order_z, kept_masks, wide_y, wide_z,
    send_a, send_b, got_a, got_b, got_maps, got_coils, got_times, got_mask, ytab, ztab,
    p_maps, p_coils, s_maps, s_coils, g_maps, g_coils,
    back_a, back_b, ret_a, ret_b, sums, got_sums,
    send_m, got_m, back_m, part_m, total_m, ret_m,
    a_out, a_in, b_out, b_in, ra_out, ra_in, rb_out, rb_in, sum_out, sum_in,
    m_out, m_in, rm_out, rm_in, fm_out, fm_in, pm_out, pm_in,
    map_out, map_in, coil_out, coil_in, time_out, time_in, mask_out, mask_in, pair_out, pair_in, own,
):
    total = n_ti * n_kz
    ti = lax.axis_index("ti")
    kz = lax.axis_index("kz")
    me = ti * n_kz + kz
    group = lax.rem(ti, COIL_GROUPS)
    half = ti // COIL_GROUPS
    n_half = n_ti // COIL_GROUPS
    first = half * COIL_GROUPS
    spot = half * n_kz + kz
    core = lax.rem(kz, 2)
    pair = kz + 1 - 2 * core
    width = dir_maps.shape[2]
    rows = dir_maps.shape[3]
    nz, ny = mask.shape[1:]
    tiles = ny // LANES
    per_tile = LANES // width
    my_coils = pl.ds(group * per_group, per_group)

    early = [
        pltpu.make_async_copy(dir_maps_in, dir_maps, own.at[6]),
        pltpu.make_async_copy(dir_coils_in, dir_coils, own.at[7]),
    ]
    for copy in early:
        copy.start()

    barrier = pltpu.get_barrier_semaphore()

    def greet(offset, carry):
        other = lax.rem(me + offset, total)
        pl.semaphore_signal(
            barrier, inc=1, device_id=(other // n_kz, lax.rem(other, n_kz)), device_id_type=MESH
        )
        return carry

    lax.fori_loop(1, total, greet, 0)

    locals_ = [
        pltpu.make_async_copy(maps.at[:, kz], got_maps.at[kz], own.at[0]),
        pltpu.make_async_copy(coils.at[:, my_coils, kz], got_coils.at[kz], own.at[1]),
        pltpu.make_async_copy(mask, got_mask.at[group], own.at[3]),
        pltpu.make_async_copy(tables_y_in, wide_y, own.at[4]),
        pltpu.make_async_copy(tables_z_in, wide_z, own.at[5]),
        pltpu.make_async_copy(res_maps_in, res_maps, own.at[2]),
        pltpu.make_async_copy(res_coils_in, res_coils, own.at[8]),
    ]
    for copy in locals_:
        copy.start()
    for b in range(2):
        times[b] = jnp.full((8, LANES), bin_times[b], jnp.float32)
        got_times[group, b] = jnp.full((8, LANES), bin_times[b], jnp.float32)
    for copy in early:
        copy.wait()

    for x in range(n_kz):
        send_m[x] = fold([dir_maps[m, x] for m in range(3)], width)
        for g in range(COIL_GROUPS):
            c = g * per_group
            send_a[x, g] = fold([dir_coils[0, c, x], dir_coils[1, c, x]], width)
            send_b[x, g] = fold([dir_coils[0, c + 1, x], dir_coils[1, c + 1, x]], width)
    got_a[me] = send_a[kz, group]
    got_b[me] = send_b[kz, group]
    got_m[group, spot] = send_m[kz]

    pl.semaphore_wait(barrier, total - 1)

    def remote(src, dst, out_sem, in_sem, where):
        return pltpu.make_async_remote_copy(src, dst, out_sem, in_sem, device_id=where, device_id_type=MESH)

    def split_id(other):
        return other // n_kz, lax.rem(other, n_kz)

    def a_copy(other, slot):
        t, k = split_id(other)
        return remote(send_a.at[k, lax.rem(t, COIL_GROUPS)], got_a.at[slot], a_out.at[other], a_in.at[slot], (t, k))

    def b_copy(other, slot):
        t, k = split_id(other)
        return remote(send_b.at[k, lax.rem(t, COIL_GROUPS)], got_b.at[slot], b_out.at[other], b_in.at[slot], (t, k))

    def ra_copy(other, slot):
        return remote(back_a.at[other], ret_a.at[slot], ra_out.at[other], ra_in.at[slot], split_id(other))

    def rb_copy(other, slot):
        return remote(back_b.at[other], ret_b.at[slot], rb_out.at[other], rb_in.at[slot], split_id(other))

    def sum_copy(other, slot):
        return remote(sums, got_sums.at[slot], sum_out.at[other], sum_in.at[slot], split_id(other))

    def send_all(copy):
        def body(offset, carry):
            copy(lax.rem(me + offset, total), me).start()
            return carry

        lax.fori_loop(1, total, body, 0)

    def wait_all(copy):
        def body(offset, carry):
            other = lax.rem(me + offset, total)
            one_copy = copy(other, other)
            one_copy.wait_send()
            one_copy.wait_recv()
            return carry

        lax.fori_loop(1, total, body, 0)

    def point_copies(other, slot):
        return [
            remote(maps.at[:, other], got_maps.at[slot], map_out.at[other], map_in.at[slot], (ti, other)),
            remote(coils.at[:, my_coils, other], got_coils.at[slot], coil_out.at[other], coil_in.at[slot], (ti, other)),
        ]

    def bin_copies(other, slot):
        where = (first + other, kz)
        return [
            remote(times, got_times.at[slot], time_out.at[other], time_in.at[slot], where),
            remote(mask.at[core], got_mask.at[slot, core], mask_out.at[other], mask_in.at[slot], where),
        ]

    def pair_copy(slot, plane):
        where = (ti, pair)
        return remote(got_mask.at[slot, plane], got_mask.at[slot, plane], pair_out.at[slot], pair_in.at[slot], where)

    def m_copy(other, slot):
        h, k = split_id(other)
        where = (h * COIL_GROUPS + group, k)
        return remote(send_m.at[k], got_m.at[group, slot], m_out.at[other], m_in.at[slot], where)

    def rm_copy(other, slot):
        h, k = split_id(other)
        where = (h * COIL_GROUPS + group, k)
        return remote(total_m.at[other], ret_m.at[slot], rm_out.at[other], rm_in.at[slot], where)

    def fm_copy(other, slot):
        return remote(got_m.at[slot], got_m.at[slot], fm_out.at[other], fm_in.at[slot], (first + other, kz))

    def pm_copy(other, slot):
        return remote(back_m.at[other], part_m.at[slot], pm_out.at[other], pm_in.at[slot], (first + other, kz))

    spots = n_half * n_kz
    for offset in range(1, spots):
        m_copy(lax.rem(spot + offset, spots), spot).start()
    send_all(a_copy)
    for offset in range(1, n_kz):
        for copy in point_copies(lax.rem(kz + offset, n_kz), kz):
            copy.start()
    for offset in range(1, spots):
        other = lax.rem(spot + offset, spots)
        m_copy(other, other).wait_send()
        m_copy(other, other).wait_recv()
    for offset in range(1, COIL_GROUPS):
        fm_copy(lax.rem(group + offset, COIL_GROUPS), group).start()
    for offset in range(1, COIL_GROUPS):
        for copy in bin_copies(lax.rem(group + offset, COIL_GROUPS), group):
            copy.start()
    send_all(b_copy)

    for copy in locals_:
        copy.wait()
    order_y[...] = even_then_odd(ny, 0)
    order_z[...] = even_then_odd(nz, 1)
    for way in range(2):
        for parity in range(2):
            high, low = halves(wide_y[way, parity])
            ytab[way, parity, 0] = high
            ytab[way, parity, 1] = low
            high, low = halves(wide_z[way, parity])
            ztab[way, parity, :nz] = high
            ztab[way, parity, nz:] = low
    for offset in range(1, n_kz):
        other = lax.rem(kz + offset, n_kz)
        for copy in point_copies(other, other):
            copy.wait_send()
            copy.wait_recv()
    for k in range(n_kz):
        span = slice(k * rows, (k + 1) * rows)
        for m in range(3):
            p_maps[m, span, :] = got_maps[k, m]
        for c in range(per_group):
            for ri in range(2):
                p_coils[2 * c + ri, span, :] = got_coils[k, ri, c]
    wait_all(a_copy)
    for offset in range(1, COIL_GROUPS):
        other = lax.rem(group + offset, COIL_GROUPS)
        fm_copy(other, group).wait_send()
        fm_copy(other, other).wait_recv()

    def store_to(targets, k, h):
        def store(p, span, value):
            ref, plane = targets[p]
            ref[plane, k * rows + span.start : k * rows + span.stop, h * LANES : (h + 1) * LANES] = value

        return store

    coil_zero = [(s_coils, 0), (s_coils, 1)]
    coil_one = [(s_coils, 2), (s_coils, 3)]
    for k in range(n_kz):
        for h in range(tiles):
            sources = [(h * per_tile + j) * n_kz + k for j in range(per_tile)]
            scatter_lanes([got_a[s] for s in sources], 2, rows, width, store_to(coil_zero, k, h))
            parts_m = []
            for j in range(per_tile):
                t = h * per_tile + j
                parts_m.append(got_m[t % COIL_GROUPS, (t // COIL_GROUPS) * n_kz + k])
            scatter_lanes(parts_m, 3, rows, width, store_to([(s_maps, m) for m in range(3)], k, h))

    g_maps[...] = jnp.zeros_like(g_maps)
    g_coils[...] = jnp.zeros_like(g_coils)

    def coil_pass(c):
        def body(offset, carry):
            other = lax.rem(group + offset, COIL_GROUPS)
            if c == 0:
                if not isinstance(offset, int):
                    pair_copy(other, core).wait_send()
                    pair_copy(other, 1 - core).wait_recv()
                bits = jnp.concatenate([got_mask[other, 0], got_mask[other, 1]], axis=0)
                bits = dot(bits.astype(jnp.float32).astype(jnp.bfloat16), order_y[...])
                bits = jnp.concatenate([bits[:nz], bits[nz:]], axis=1).astype(jnp.bfloat16)
                kept_masks[other] = dot(order_z[...], bits)

            amplitude = p_maps[1]
            model = []
            rows_in = []
            for b in range(2):
                tau = got_times[other, b, 0:1, 0:1]
                decays = jnp.exp(-tau * p_maps[2])
                signal = p_maps[0] - amplitude * decays
                slope = amplitude * tau * decays
                signal_step = s_maps[0] - s_maps[1] * decays + slope * s_maps[2]
                real = p_coils[2 * c] * signal_step + s_coils[2 * c] * signal
                imag = p_coils[2 * c + 1] * signal_step + s_coils[2 * c + 1] * signal
                rows_in.append(jnp.concatenate([real, imag], axis=1))
                model.append((decays, signal, slope))
            x = jnp.concatenate(rows_in, axis=0)
            h = ny // 2
            left, right = [jnp.concatenate([x[:, o : o + h], x[:, ny + o : ny + o + h]], axis=1) for o in (0, h)]
            even = from_right(left + right, ytab[0, 0])
            odd = from_right(left - right, ytab[0, 1])
            parts_z = []
            for o in (0, h):
                parts_z.append(
                    jnp.concatenate(
                        [
                            v
                            for b in range(2)
                            for v in (even[b * nz : (b + 1) * nz, o : o + h], odd[b * nz : (b + 1) * nz, o : o + h])
                        ],
                        axis=1,
                    )
                )
            q = nz // 2
            top = jnp.concatenate([v[:q] for v in parts_z], axis=0)
            bottom = jnp.concatenate([v[q:] for v in parts_z], axis=0)
            kept_even = kept_masks[other, :q]
            kept_odd = kept_masks[other, q:]
            even = from_left(ztab[0, 0], top + bottom) * jnp.concatenate([kept_even] * 2, axis=0)
            odd = from_left(ztab[0, 1], top - bottom) * jnp.concatenate([kept_odd] * 2, axis=0)
            even = from_left(ztab[1, 0], even)
            odd = from_left(ztab[1, 1], odd)
            top, bottom = even + odd, even - odd
            real = jnp.concatenate([top[:q], bottom[:q]], axis=0)
            imag = jnp.concatenate([top[q:], bottom[q:]], axis=0)
            even, odd = [
                jnp.concatenate(
                    [
                        jnp.concatenate([v[:, b * ny + o : b * ny + o + h] for v in (real, imag)], axis=1)
                        for b in range(2)
                    ],
                    axis=0,
                )
                for o in (0, h)
            ]
            even = from_right(even, ytab[1, 0])
            odd = from_right(odd, ytab[1, 1])
            left, right = even + odd, even - odd
            for b, (decays, signal, slope) in enumerate(model):
                span = slice(b * nz, (b + 1) * nz)
                real = jnp.concatenate([left[span, :h], right[span, :h]], axis=1)
                imag = jnp.concatenate([left[span, h:], right[span, h:]], axis=1)
                projected = p_coils[2 * c] * real + p_coils[2 * c + 1] * imag
                g_coils[2 * c] += signal * real
                g_coils[2 * c + 1] += signal * imag
                g_maps[0] += projected
                g_maps[1] -= decays * projected
                g_maps[2] += slope * projected
            return carry

        if c == 0:
            body(0, 0)
            for offset in range(1, COIL_GROUPS):
                other = lax.rem(group + offset, COIL_GROUPS)
                for copy in bin_copies(other, other):
                    copy.wait_send()
                    copy.wait_recv()
                pair_copy(other, core).start()
            lax.fori_loop(1, COIL_GROUPS, body, 0)
        else:
            lax.fori_loop(0, COIL_GROUPS, body, 0)

    coil_pass(0)

    for k in range(n_kz):
        span = slice(k * rows, (k + 1) * rows)
        for h in range(tiles):
            lanes = slice(h * LANES, (h + 1) * LANES)
            planes = [g_coils[p, span, lanes] for p in range(2)]
            for j in range(per_tile):
                back_b[(h * per_tile + j) * n_kz + k] = collect_lanes(planes, j, rows, width)
    send_all(rb_copy)
    ret_b[me] = back_b[me]

    wait_all(b_copy)
    for k in range(n_kz):
        for h in range(tiles):
            sources = [(h * per_tile + j) * n_kz + k for j in range(per_tile)]
            scatter_lanes([got_b[s] for s in sources], 2, rows, width, store_to(coil_one, k, h))

    coil_pass(1)

    for k in range(n_kz):
        span = slice(k * rows, (k + 1) * rows)
        for h in range(tiles):
            lanes = slice(h * LANES, (h + 1) * LANES)
            planes = [g_maps[m, span, lanes] for m in range(3)]
            for j in range(per_tile):
                t = h * per_tile + j
                back_m[t % COIL_GROUPS, (t // COIL_GROUPS) * n_kz + k] = collect_lanes(planes, j, rows, width)
    for offset in range(1, COIL_GROUPS):
        pm_copy(lax.rem(group + offset, COIL_GROUPS), group).start()
    for k in range(n_kz):
        span = slice(k * rows, (k + 1) * rows)
        for h in range(tiles):
            lanes = slice(h * LANES, (h + 1) * LANES)
            planes = [g_coils[p, span, lanes] for p in (2, 3)]
            for j in range(per_tile):
                back_a[(h * per_tile + j) * n_kz + k] = collect_lanes(planes, j, rows, width)
    send_all(ra_copy)
    ret_a[me] = back_a[me]
    others = [lax.rem(group + offset, COIL_GROUPS) for offset in range(1, COIL_GROUPS)]
    for other in others:
        pm_copy(other, group).wait_send()
        pm_copy(other, other).wait_recv()
    total_m[...] = (back_m[group] + part_m[others[0]]) + (part_m[others[1]] + part_m[others[2]])
    for offset in range(1, spots):
        rm_copy(lax.rem(spot + offset, spots), spot).start()
    ret_m[spot] = total_m[spot]
    wait_all(rb_copy)

    parts = {"old": None, "bend": None, "cross": None, "square": None}

    def settle(applied, grad, d, r):
        a = grad + regular_weight * d
        for key, value in (("old", r * r), ("bend", d * a), ("cross", r * a), ("square", a * a)):
            parts[key] = value if parts[key] is None else parts[key] + value
        return a

    def settle_coils(c, x, flat):
        for ri in range(2):
            grad = flat[ri * width : (ri + 1) * width]
            app_coils[ri, c, x] = settle(None, grad, dir_coils[ri, c, x], res_coils[ri, c, x])

    def added(terms):
        return functools.reduce(lambda u, v: u + v, terms)

    for x in range(n_kz):
        for g in range(COIL_GROUPS):
            block = added([ret_b[t * n_kz + x] for t in range(g, n_ti, COIL_GROUPS)])
            settle_coils(g * per_group, x, unfold(block, 2, rows, width))

    wait_all(ra_copy)
    for x in range(n_kz):
        for g in range(COIL_GROUPS):
            block = added([ret_a[t * n_kz + x] for t in range(g, n_ti, COIL_GROUPS)])
            settle_coils(g * per_group + 1, x, unfold(block, 2, rows, width))
    for offset in range(1, spots):
        other = lax.rem(spot + offset, spots)
        rm_copy(other, other).wait_send()
        rm_copy(other, other).wait_recv()
    for x in range(n_kz):
        flat = unfold(added([ret_m[h * n_kz + x] for h in range(n_half)]), 3, rows, width)
        grads = [flat[m * width : (m + 1) * width] for m in range(3)]
        for m, grad in enumerate(grads):
            app_maps[m, x] = settle(None, grad, dir_maps[m, x], res_maps[m, x])

    row = lax.broadcasted_iota(jnp.int32, sums.shape, 0)
    tile = jnp.zeros(sums.shape, jnp.float32)
    for i, part in enumerate(parts.values()):
        tile = jnp.where(row == i, jnp.sum(part, keepdims=True), tile)
    sums[...] = tile
    send_all(sum_copy)
    got_sums[me] = tile
    wait_all(sum_copy)
    whole = jnp.sum(got_sums[...], axis=0)
    old, bend, cross, square = (whole[i : i + 1, :] for i in range(4))
    step = old / bend
    ratio = (old - 2.0 * step * cross + step * step * square) / old
    scales[0] = jnp.broadcast_to(step, scales.shape[1:])
    scales[1] = jnp.broadcast_to(ratio, scales.shape[1:])


def finish_kernel(scales, app_maps, app_coils, dir_maps, dir_coils, res_maps, res_coils, *outs):
    step = scales[0, 0:1, 0 : app_maps.shape[-1]]
    ratio = scales[1, 0:1, 0 : app_maps.shape[-1]]
    for i, (applied, d, r) in enumerate(((app_maps, dir_maps, res_maps), (app_coils, dir_coils, res_coils))):
        updated = r[...] - step * applied[...]
        outs[i][...] = updated
        outs[2 + i][...] = updated + ratio * d[...]


def shards(
    n_ti, n_kz,
    point_maps, point_coils, direction_maps, direction_coils,
    residual_maps, residual_coils, inversion_times, sampling_mask,
):
    total = n_ti * n_kz
    coils = point_coils.shape[1]
    per_group = coils // COIL_GROUPS
    rows, ny = point_maps.shape[2:]
    width = ny // n_ti
    local_bins, nz, _ = sampling_mask.shape
    f32 = jnp.float32
    vmem = pl.BlockSpec(memory_space=pltpu.VMEM)
    dma = pltpu.SemaphoreType.DMA
    hbm = pl.BlockSpec(memory_space=pltpu.HBM)
    tables = [jnp.asarray(t) for t in (tables_y(ny), tables_z(nz))]
    flipped = [
        jnp.swapaxes(a, -1, -2) for a in (direction_maps, direction_coils, residual_maps, residual_coils)
    ]
    two, three = (lane_spans(rows, planes, width)[0] for planes in (2, 3))
    spots = (n_ti // COIL_GROUPS) * n_kz
    x_maps = pltpu.VMEM((COIL_GROUPS, spots, three, LANES), f32)
    y_maps = pltpu.VMEM((spots, three, LANES), f32)

    outs = pl.pallas_call(
        functools.partial(step_kernel, n_ti, n_kz, per_group),
        out_shape=[jax.ShapeDtypeStruct(shape, f32) for shape in (flipped[0].shape, flipped[1].shape, (2, 8, LANES))],
        in_specs=[hbm] * 6 + [pl.BlockSpec(memory_space=pltpu.SMEM)] + [hbm] * 3,
        out_specs=[vmem] * 3,
        scratch_shapes=[
            *(pltpu.VMEM(a.shape, f32) for a in flipped),
            pltpu.VMEM((local_bins, 8, LANES), f32),
            pltpu.VMEM((ny, ny), jnp.bfloat16),
            pltpu.VMEM((nz, nz), jnp.bfloat16),
            pltpu.VMEM((COIL_GROUPS, nz, 2 * ny), f32),
            *(pltpu.VMEM(t.shape, f32) for t in tables),
            pltpu.VMEM((n_kz, COIL_GROUPS, two, LANES), f32),
            pltpu.VMEM((n_kz, COIL_GROUPS, two, LANES), f32),
            pltpu.VMEM((total, two, LANES), f32),
            pltpu.VMEM((total, two, LANES), f32),
            pltpu.VMEM((n_kz, 3, rows, ny), f32),
            pltpu.VMEM((n_kz, 2, per_group, rows, ny), f32),
            pltpu.VMEM((COIL_GROUPS, local_bins, 8, LANES), f32),
            pltpu.VMEM((COIL_GROUPS,) + sampling_mask.shape, jnp.int32),
            pltpu.VMEM((2, 2, 2, ny, ny), jnp.bfloat16),
            pltpu.VMEM((2, 2, 2 * nz, nz), jnp.bfloat16),
            pltpu.VMEM((3, nz, ny), f32),
            pltpu.VMEM((2 * per_group, nz, ny), f32),
            pltpu.VMEM((3, nz, ny), f32),
            pltpu.VMEM((2 * per_group, nz, ny), f32),
            pltpu.VMEM((3, nz, ny), f32),
            pltpu.VMEM((2 * per_group, nz, ny), f32),
            pltpu.VMEM((total, two, LANES), f32),
            pltpu.VMEM((total, two, LANES), f32),
            pltpu.VMEM((total, two, LANES), f32),
            pltpu.VMEM((total, two, LANES), f32),
            pltpu.VMEM((8, LANES), f32),
            pltpu.VMEM((total, 8, LANES), f32),
            pltpu.VMEM((n_kz, three, LANES), f32),
            x_maps, x_maps, x_maps, y_maps, y_maps,
        ]
        + [dma((total,))] * 10
        + [dma((spots,))] * 4
        + [dma((COIL_GROUPS,))] * 4
        + [dma((n_kz,))] * 4
        + [dma((COIL_GROUPS,))] * 6
        + [dma((9,))],
        compiler_params=pltpu.CompilerParams(
            collective_id=0, has_side_effects=True, vmem_limit_bytes=VMEM_LIMIT
        ),
        name="step",
    )(*flipped, point_maps, point_coils, inversion_times, sampling_mask, *tables)
    maps_block = pl.BlockSpec((3, 1, width, rows), lambda x: (0, x, 0, 0))
    coils_block = pl.BlockSpec((2, coils, 1, width, rows), lambda x: (0, 0, x, 0, 0))
    updated = pl.pallas_call(
        finish_kernel,
        out_shape=[jax.ShapeDtypeStruct(flipped[i].shape, f32) for i in (0, 1, 0, 1)],
        grid=(n_kz,),
        in_specs=[pl.BlockSpec((2, 8, LANES), lambda x: (0, 0, 0))] + [maps_block, coils_block] * 3,
        out_specs=[maps_block, coils_block] * 2,
        compiler_params=pltpu.CompilerParams(vmem_limit_bytes=VMEM_LIMIT),
        name="finish",
    )(outs[2], outs[0], outs[1], *flipped)
    return tuple(jnp.swapaxes(a, -1, -2) for a in updated)


def solution(mesh):
    in_specs = (
        P(None, None, "kz", None),
        P(None, None, None, "kz", None),
        P(None, None, "kz", "ti"),
        P(None, None, None, "kz", "ti"),
        P(None, None, "kz", "ti"),
        P(None, None, None, "kz", "ti"),
        P("ti"),
        P("ti", None, None),
    )
    out_specs = (
        P(None, None, "kz", "ti"),
        P(None, None, None, "kz", "ti"),
        P(None, None, "kz", "ti"),
        P(None, None, None, "kz", "ti"),
    )
    body = functools.partial(shards, mesh.shape["ti"], mesh.shape["kz"])
    return jax.shard_map(body, mesh=mesh, in_specs=in_specs, out_specs=out_specs, check_vma=False)
```

```python
import functools
import math

import jax
import jax.numpy as jnp
import numpy as np
from jax import lax
from jax.experimental import pallas as pl
from jax.experimental.pallas import tpu as pltpu
from jax.sharding import PartitionSpec as P

MESH = pl.DeviceIdType.MESH
regular_weight = 2.0
COIL_GROUPS = 4
LANES = 128
VMEM_LIMIT = 59 * 1024 * 1024


def half_parts(length, parity):
    points = np.arange(length // 2)
    orders = 2 * points + parity
    angles = (points[:, None] * orders[None, :] % length) * (2.0 * math.pi / length)
    factor = 1.0 / math.sqrt(length)
    return np.cos(angles) * factor, np.sin(angles) * factor


def tables_y(length):
    forward, backward = [], []
    for parity in range(2):
        c, s = half_parts(length, parity)
        forward.append(np.block([[c, -s], [s, c]]))
        backward.append(np.block([[c.T, s.T], [-s.T, c.T]]))
    return np.stack([np.stack(forward), np.stack(backward)]).astype(np.float32)


def tables_z(length):
    forward, backward = [], []
    for parity in range(2):
        c, s = half_parts(length, parity)
        forward.append(np.block([[c.T, s.T], [-s.T, c.T]]))
        backward.append(np.block([[c, -s], [s, c]]))
    return np.stack([np.stack(forward), np.stack(backward)]).astype(np.float32)


def even_then_odd(length, source_axis):
    source = lax.broadcasted_iota(jnp.int32, (length, length), source_axis)
    place = lax.broadcasted_iota(jnp.int32, (length, length), 1 - source_axis)
    wanted = jnp.where(place < length // 2, 2 * place, 2 * place - length + 1)
    return jnp.where(source == wanted, 1.0, 0.0).astype(jnp.bfloat16)


def halves(values):
    high = values.astype(jnp.bfloat16)
    low = (values - high.astype(jnp.float32)).astype(jnp.bfloat16)
    return high, low


dot = functools.partial(jnp.dot, preferred_element_type=jnp.float32)


def from_right(values, table):
    high, low = halves(values)
    return dot(high, table[0]) + (dot(low, table[0]) + dot(high, table[1]))


def from_left(table, values):
    high, low = halves(values)
    size = table.shape[1]
    both = dot(table, high)
    return both[:size] + (both[size:] + dot(table[:size], low))


def lane_spans(rows, planes, width):
    count = LANES // (planes * width)
    chunk = -(-(-(-rows // count)) // 8) * 8
    return chunk, [(start, min(chunk, rows - start)) for start in range(0, rows, chunk)]


def lane_blocks(rows, width):
    return lax.broadcasted_iota(jnp.int32, (rows, LANES), 1) // width


def turned(values, shift):
    shift %= LANES
    return pltpu.roll(values, shift, 1) if shift else values


def tall(values, rows):
    missing = rows - values.shape[0]
    if missing:
        values = jnp.concatenate([values, jnp.zeros((missing,) + values.shape[1:], values.dtype)], axis=0)
    return values


def fold(parts, width):
    rows = parts[0].shape[1]
    planes = len(parts)
    chunk, spans = lane_spans(rows, planes, width)
    block = tall(jnp.concatenate(parts, axis=0), LANES).T
    if len(spans) == 1:
        return tall(block, chunk)
    ids = lane_blocks(chunk, planes * width)
    value = jnp.zeros((chunk, LANES), jnp.float32)
    for i, (start, size) in enumerate(spans):
        moved = turned(tall(block[start : start + size], chunk), i * planes * width)
        value = jnp.where(ids == i, moved, value)
    return value


def unfold(block, planes, rows, width):
    _, spans = lane_spans(rows, planes, width)
    parts = [turned(block[:size], -i * planes * width) for i, (_, size) in enumerate(spans)]
    return (jnp.concatenate(parts, axis=0) if len(parts) > 1 else parts[0]).T


def scatter_lanes(blocks, planes, rows, width, store):
    _, spans = lane_spans(rows, planes, width)
    for p in range(planes):
        for i, (start, size) in enumerate(spans):
            ids = lane_blocks(size, width)
            value = None
            for j, block in enumerate(blocks):
                moved = turned(block[:size], (j - i * planes - p) * width)
                value = moved if value is None else jnp.where(ids == j, moved, value)
            store(p, slice(start, start + size), value)


def collect_lanes(planes, j, rows, width):
    chunk, spans = lane_spans(rows, len(planes), width)
    ids = lane_blocks(chunk, width)
    value = jnp.zeros((chunk, LANES), jnp.float32)
    for p, plane in enumerate(planes):
        for i, (start, size) in enumerate(spans):
            q = i * len(planes) + p
            moved = turned(tall(plane[start : start + size], chunk), (q - j) * width)
            value = jnp.where(ids == q, moved, value)
    return value


def step_kernel(
    n_ti, n_kz, per_group,
    dir_maps_in, dir_coils_in, res_maps_in, res_coils_in, maps, coils, bin_times, mask,
    tables_y_in, tables_z_in,
    app_maps, app_coils, scales,
    dir_maps, dir_coils, res_maps, res_coils, times, order_y, order_z, kept_masks, wide_y, wide_z,
    send_a, send_b, got_a, got_b, got_maps, got_coils, got_times, got_mask, ytab, ztab,
    p_maps, p_coils, s_maps, s_coils, g_maps, g_coils,
    back_a, back_b, ret_a, ret_b, sums, got_sums,
    send_m, got_m, back_m, part_m, total_m, ret_m,
    a_out, a_in, b_out, b_in, ra_out, ra_in, rb_out, rb_in, sum_out, sum_in,
    m_out, m_in, rm_out, rm_in, fm_out, fm_in, pm_out, pm_in,
    map_out, map_in, coil_out, coil_in, time_out, time_in, mask_out, mask_in, pair_out, pair_in, own,
):
    total = n_ti * n_kz
    ti = lax.axis_index("ti")
    kz = lax.axis_index("kz")
    me = ti * n_kz + kz
    group = lax.rem(ti, COIL_GROUPS)
    half = ti // COIL_GROUPS
    n_half = n_ti // COIL_GROUPS
    first = half * COIL_GROUPS
    spot = half * n_kz + kz
    core = lax.rem(kz, 2)
    pair = kz + 1 - 2 * core
    width = dir_maps.shape[2]
    rows = dir_maps.shape[3]
    nz, ny = mask.shape[1:]
    tiles = ny // LANES
    per_tile = LANES // width
    my_coils = pl.ds(group * per_group, per_group)

    early = [
        pltpu.make_async_copy(dir_maps_in, dir_maps, own.at[6]),
        pltpu.make_async_copy(dir_coils_in, dir_coils, own.at[7]),
    ]
    for copy in early:
        copy.start()

    barrier = pltpu.get_barrier_semaphore()

    def greet(offset, carry):
        other = lax.rem(me + offset, total)
        pl.semaphore_signal(
            barrier, inc=1, device_id=(other // n_kz, lax.rem(other, n_kz)), device_id_type=MESH
        )
        return carry

    lax.fori_loop(1, total, greet, 0)

    locals_ = [
        pltpu.make_async_copy(maps.at[:, kz], got_maps.at[kz], own.at[0]),
        pltpu.make_async_copy(coils.at[:, my_coils, kz], got_coils.at[kz], own.at[1]),
        pltpu.make_async_copy(mask, got_mask.at[group], own.at[3]),
        pltpu.make_async_copy(tables_y_in, wide_y, own.at[4]),
        pltpu.make_async_copy(tables_z_in, wide_z, own.at[5]),
        pltpu.make_async_copy(res_maps_in, res_maps, own.at[2]),
        pltpu.make_async_copy(res_coils_in, res_coils, own.at[8]),
    ]
    for copy in locals_:
        copy.start()
    for b in range(2):
        times[b] = jnp.full((8, LANES), bin_times[b], jnp.float32)
        got_times[group, b] = jnp.full((8, LANES), bin_times[b], jnp.float32)
    for copy in early:
        copy.wait()

    for x in range(n_kz):
        send_m[x] = fold([dir_maps[m, x] for m in range(3)], width)
        for g in range(COIL_GROUPS):
            c = g * per_group
            send_a[x, g] = fold([dir_coils[0, c, x], dir_coils[1, c, x]], width)
    got_a[me] = send_a[kz, group]
    got_m[group, spot] = send_m[kz]

    pl.semaphore_wait(barrier, total - 1)

    def remote(src, dst, out_sem, in_sem, where):
        return pltpu.make_async_remote_copy(src, dst, out_sem, in_sem, device_id=where, device_id_type=MESH)

    def split_id(other):
        return other // n_kz, lax.rem(other, n_kz)

    def a_copy(other, slot):
        t, k = split_id(other)
        return remote(send_a.at[k, lax.rem(t, COIL_GROUPS)], got_a.at[slot], a_out, a_in, (t, k))

    def b_copy(other, slot):
        t, k = split_id(other)
        return remote(send_b.at[k, lax.rem(t, COIL_GROUPS)], got_b.at[slot], b_out, b_in, (t, k))

    def ra_copy(other, slot):
        return remote(back_a.at[other], ret_a.at[slot], ra_out, ra_in, split_id(other))

    def rb_copy(other, slot):
        return remote(back_b.at[other], ret_b.at[slot], rb_out, rb_in, split_id(other))

    def sum_copy(other, slot):
        return remote(sums, got_sums.at[slot], sum_out, sum_in, split_id(other))

    def send_all(copy):
        def body(offset, carry):
            copy(lax.rem(me + offset, total), me).start()
            return carry

        lax.fori_loop(1, total, body, 0)

    def wait_bytes(slots, sem):
        part = slots.at[pl.ds(0, total - 1)]
        pltpu.make_async_copy(part, part, sem).wait()

    def point_copies(other, slot):
        return [
            remote(maps.at[:, other], got_maps.at[slot], map_out.at[other], map_in.at[slot], (ti, other)),
            remote(coils.at[:, my_coils, other], got_coils.at[slot], coil_out.at[other], coil_in.at[slot], (ti, other)),
        ]

    def bin_copies(other, slot):
        where = (first + other, kz)
        return [
            remote(times, got_times.at[slot], time_out.at[other], time_in.at[slot], where),
            remote(mask.at[core], got_mask.at[slot, core], mask_out.at[other], mask_in.at[slot], where),
        ]

    def pair_copy(slot, plane):
        where = (ti, pair)
        return remote(got_mask.at[slot, plane], got_mask.at[slot, plane], pair_out.at[slot], pair_in.at[slot], where)

    def m_copy(other, slot):
        h, k = split_id(other)
        where = (h * COIL_GROUPS + group, k)
        return remote(send_m.at[k], got_m.at[group, slot], m_out.at[other], m_in.at[slot], where)

    def rm_copy(other, slot):
        h, k = split_id(other)
        where = (h * COIL_GROUPS + group, k)
        return remote(total_m.at[other], ret_m.at[slot], rm_out.at[other], rm_in.at[slot], where)

    def fm_copy(other, slot):
        return remote(got_m.at[slot], got_m.at[slot], fm_out.at[other], fm_in.at[slot], (first + other, kz))

    def pm_copy(other, slot):
        return remote(back_m.at[other], part_m.at[slot], pm_out.at[other], pm_in.at[slot], (first + other, kz))

    spots = n_half * n_kz
    for offset in range(1, spots):
        m_copy(lax.rem(spot + offset, spots), spot).start()
    send_all(a_copy)
    for offset in range(1, n_kz):
        for copy in point_copies(lax.rem(kz + offset, n_kz), kz):
            copy.start()
    for x in range(n_kz):
        for g in range(COIL_GROUPS):
            c = g * per_group + 1
            send_b[x, g] = fold([dir_coils[0, c, x], dir_coils[1, c, x]], width)
    got_b[me] = send_b[kz, group]
    for offset in range(1, spots):
        other = lax.rem(spot + offset, spots)
        m_copy(other, other).wait_send()
        m_copy(other, other).wait_recv()
    for offset in range(1, COIL_GROUPS):
        fm_copy(lax.rem(group + offset, COIL_GROUPS), group).start()
    for offset in range(1, COIL_GROUPS):
        for copy in bin_copies(lax.rem(group + offset, COIL_GROUPS), group):
            copy.start()
    send_all(b_copy)

    for copy in locals_:
        copy.wait()
    order_y[...] = even_then_odd(ny, 0)
    order_z[...] = even_then_odd(nz, 1)
    for way in range(2):
        for parity in range(2):
            high, low = halves(wide_y[way, parity])
            ytab[way, parity, 0] = high
            ytab[way, parity, 1] = low
            high, low = halves(wide_z[way, parity])
            ztab[way, parity, :nz] = high
            ztab[way, parity, nz:] = low
    for offset in range(1, n_kz):
        other = lax.rem(kz + offset, n_kz)
        for copy in point_copies(other, other):
            copy.wait_send()
            copy.wait_recv()
    for k in range(n_kz):
        span = slice(k * rows, (k + 1) * rows)
        for m in range(3):
            p_maps[m, span, :] = got_maps[k, m]
        for c in range(per_group):
            for ri in range(2):
                p_coils[2 * c + ri, span, :] = got_coils[k, ri, c]
    wait_bytes(got_a, a_in)
    for offset in range(1, COIL_GROUPS):
        other = lax.rem(group + offset, COIL_GROUPS)
        fm_copy(other, group).wait_send()
        fm_copy(other, other).wait_recv()

    def store_to(targets, k, h):
        def store(p, span, value):
            ref, plane = targets[p]
            ref[plane, k * rows + span.start : k * rows + span.stop, h * LANES : (h + 1) * LANES] = value

        return store

    coil_zero = [(s_coils, 0), (s_coils, 1)]
    coil_one = [(s_coils, 2), (s_coils, 3)]
    for k in range(n_kz):
        for h in range(tiles):
            sources = [(h * per_tile + j) * n_kz + k for j in range(per_tile)]
            scatter_lanes([got_a[s] for s in sources], 2, rows, width, store_to(coil_zero, k, h))
            parts_m = []
            for j in range(per_tile):
                t = h * per_tile + j
                parts_m.append(got_m[t % COIL_GROUPS, (t // COIL_GROUPS) * n_kz + k])
            scatter_lanes(parts_m, 3, rows, width, store_to([(s_maps, m) for m in range(3)], k, h))

    g_maps[...] = jnp.zeros_like(g_maps)
    g_coils[...] = jnp.zeros_like(g_coils)

    def coil_pass(c):
        def body(offset, carry):
            other = lax.rem(group + offset, COIL_GROUPS)
            if c == 0:
                if not isinstance(offset, int):
                    pair_copy(other, core).wait_send()
                    pair_copy(other, 1 - core).wait_recv()
                bits = jnp.concatenate([got_mask[other, 0], got_mask[other, 1]], axis=0)
                bits = dot(bits.astype(jnp.float32).astype(jnp.bfloat16), order_y[...])
                bits = jnp.concatenate([bits[:nz], bits[nz:]], axis=1).astype(jnp.bfloat16)
                kept_masks[other] = dot(order_z[...], bits)

            amplitude = p_maps[1]
            model = []
            rows_in = []
            for b in range(2):
                tau = got_times[other, b, 0:1, 0:1]
                decays = jnp.exp(-tau * p_maps[2])
                signal = p_maps[0] - amplitude * decays
                slope = amplitude * tau * decays
                signal_step = s_maps[0] - s_maps[1] * decays + slope * s_maps[2]
                real = p_coils[2 * c] * signal_step + s_coils[2 * c] * signal
                imag = p_coils[2 * c + 1] * signal_step + s_coils[2 * c + 1] * signal
                rows_in.append(jnp.concatenate([real, imag], axis=1))
                model.append((decays, signal, slope))
            x = jnp.concatenate(rows_in, axis=0)
            h = ny // 2
            left, right = [jnp.concatenate([x[:, o : o + h], x[:, ny + o : ny + o + h]], axis=1) for o in (0, h)]
            even = from_right(left + right, ytab[0, 0])
            odd = from_right(left - right, ytab[0, 1])
            parts_z = []
            for o in (0, h):
                parts_z.append(
                    jnp.concatenate(
                        [
                            v
                            for b in range(2)
                            for v in (even[b * nz : (b + 1) * nz, o : o + h], odd[b * nz : (b + 1) * nz, o : o + h])
                        ],
                        axis=1,
                    )
                )
            q = nz // 2
            top = jnp.concatenate([v[:q] for v in parts_z], axis=0)
            bottom = jnp.concatenate([v[q:] for v in parts_z], axis=0)
            kept_even = kept_masks[other, :q]
            kept_odd = kept_masks[other, q:]
            even = from_left(ztab[0, 0], top + bottom) * jnp.concatenate([kept_even] * 2, axis=0)
            odd = from_left(ztab[0, 1], top - bottom) * jnp.concatenate([kept_odd] * 2, axis=0)
            even = from_left(ztab[1, 0], even)
            odd = from_left(ztab[1, 1], odd)
            top, bottom = even + odd, even - odd
            real = jnp.concatenate([top[:q], bottom[:q]], axis=0)
            imag = jnp.concatenate([top[q:], bottom[q:]], axis=0)
            even, odd = [
                jnp.concatenate(
                    [
                        jnp.concatenate([v[:, b * ny + o : b * ny + o + h] for v in (real, imag)], axis=1)
                        for b in range(2)
                    ],
                    axis=0,
                )
                for o in (0, h)
            ]
            even = from_right(even, ytab[1, 0])
            odd = from_right(odd, ytab[1, 1])
            left, right = even + odd, even - odd
            for b, (decays, signal, slope) in enumerate(model):
                span = slice(b * nz, (b + 1) * nz)
                real = jnp.concatenate([left[span, :h], right[span, :h]], axis=1)
                imag = jnp.concatenate([left[span, h:], right[span, h:]], axis=1)
                projected = p_coils[2 * c] * real + p_coils[2 * c + 1] * imag
                g_coils[2 * c] += signal * real
                g_coils[2 * c + 1] += signal * imag
                g_maps[0] += projected
                g_maps[1] -= decays * projected
                g_maps[2] += slope * projected
            return carry

        if c == 0:
            body(0, 0)
            for offset in range(1, COIL_GROUPS):
                other = lax.rem(group + offset, COIL_GROUPS)
                for copy in bin_copies(other, other):
                    copy.wait_send()
                    copy.wait_recv()
                pair_copy(other, core).start()
            lax.fori_loop(1, COIL_GROUPS, body, 0)
        else:
            lax.fori_loop(0, COIL_GROUPS, body, 0)

    coil_pass(0)

    for k in range(n_kz):
        span = slice(k * rows, (k + 1) * rows)
        for h in range(tiles):
            lanes = slice(h * LANES, (h + 1) * LANES)
            planes = [g_coils[p, span, lanes] for p in range(2)]
            for j in range(per_tile):
                back_b[(h * per_tile + j) * n_kz + k] = collect_lanes(planes, j, rows, width)
    send_all(rb_copy)
    ret_b[me] = back_b[me]

    wait_bytes(got_b, b_in)
    for k in range(n_kz):
        for h in range(tiles):
            sources = [(h * per_tile + j) * n_kz + k for j in range(per_tile)]
            scatter_lanes([got_b[s] for s in sources], 2, rows, width, store_to(coil_one, k, h))

    coil_pass(1)

    for k in range(n_kz):
        span = slice(k * rows, (k + 1) * rows)
        for h in range(tiles):
            lanes = slice(h * LANES, (h + 1) * LANES)
            planes = [g_maps[m, span, lanes] for m in range(3)]
            for j in range(per_tile):
                t = h * per_tile + j
                back_m[t % COIL_GROUPS, (t // COIL_GROUPS) * n_kz + k] = collect_lanes(planes, j, rows, width)
    for offset in range(1, COIL_GROUPS):
        pm_copy(lax.rem(group + offset, COIL_GROUPS), group).start()
    for k in range(n_kz):
        span = slice(k * rows, (k + 1) * rows)
        for h in range(tiles):
            lanes = slice(h * LANES, (h + 1) * LANES)
            planes = [g_coils[p, span, lanes] for p in (2, 3)]
            for j in range(per_tile):
                back_a[(h * per_tile + j) * n_kz + k] = collect_lanes(planes, j, rows, width)
    send_all(ra_copy)
    ret_a[me] = back_a[me]
    others = [lax.rem(group + offset, COIL_GROUPS) for offset in range(1, COIL_GROUPS)]
    for other in others:
        pm_copy(other, group).wait_send()
        pm_copy(other, other).wait_recv()
    total_m[...] = (back_m[group] + part_m[others[0]]) + (part_m[others[1]] + part_m[others[2]])
    for offset in range(1, spots):
        rm_copy(lax.rem(spot + offset, spots), spot).start()
    ret_m[spot] = total_m[spot]
    wait_bytes(ret_b, rb_in)

    parts = {"old": None, "bend": None, "cross": None, "square": None}

    def settle(applied, grad, d, r):
        a = grad + regular_weight * d
        for key, value in (("old", r * r), ("bend", d * a), ("cross", r * a), ("square", a * a)):
            parts[key] = value if parts[key] is None else parts[key] + value
        return a

    def settle_coils(c, x, flat):
        for ri in range(2):
            grad = flat[ri * width : (ri + 1) * width]
            app_coils[ri, c, x] = settle(None, grad, dir_coils[ri, c, x], res_coils[ri, c, x])

    def added(terms):
        return functools.reduce(lambda u, v: u + v, terms)

    for x in range(n_kz):
        for g in range(COIL_GROUPS):
            block = added([ret_b[t * n_kz + x] for t in range(g, n_ti, COIL_GROUPS)])
            settle_coils(g * per_group, x, unfold(block, 2, rows, width))

    wait_bytes(ret_a, ra_in)
    for x in range(n_kz):
        for g in range(COIL_GROUPS):
            block = added([ret_a[t * n_kz + x] for t in range(g, n_ti, COIL_GROUPS)])
            settle_coils(g * per_group + 1, x, unfold(block, 2, rows, width))
    for offset in range(1, spots):
        other = lax.rem(spot + offset, spots)
        rm_copy(other, other).wait_send()
        rm_copy(other, other).wait_recv()
    for x in range(n_kz):
        flat = unfold(added([ret_m[h * n_kz + x] for h in range(n_half)]), 3, rows, width)
        grads = [flat[m * width : (m + 1) * width] for m in range(3)]
        for m, grad in enumerate(grads):
            app_maps[m, x] = settle(None, grad, dir_maps[m, x], res_maps[m, x])

    row = lax.broadcasted_iota(jnp.int32, sums.shape, 0)
    tile = jnp.zeros(sums.shape, jnp.float32)
    for i, part in enumerate(parts.values()):
        tile = jnp.where(row == i, jnp.sum(part, keepdims=True), tile)
    sums[...] = tile
    send_all(sum_copy)
    got_sums[me] = tile
    wait_bytes(got_a, a_out)
    wait_bytes(got_b, b_out)
    wait_bytes(ret_a, ra_out)
    wait_bytes(ret_b, rb_out)
    wait_bytes(got_sums, sum_in)
    wait_bytes(got_sums, sum_out)
    whole = jnp.sum(got_sums[...], axis=0)
    old, bend, cross, square = (whole[i : i + 1, :] for i in range(4))
    step = old / bend
    ratio = (old - 2.0 * step * cross + step * step * square) / old
    scales[0] = jnp.broadcast_to(step, scales.shape[1:])
    scales[1] = jnp.broadcast_to(ratio, scales.shape[1:])


def finish_kernel(scales, app_maps, app_coils, dir_maps, dir_coils, res_maps, res_coils, *outs):
    step = scales[0, 0:1, 0 : app_maps.shape[-1]]
    ratio = scales[1, 0:1, 0 : app_maps.shape[-1]]
    for i, (applied, d, r) in enumerate(((app_maps, dir_maps, res_maps), (app_coils, dir_coils, res_coils))):
        updated = r[...] - step * applied[...]
        outs[i][...] = updated
        outs[2 + i][...] = updated + ratio * d[...]


def shards(
    n_ti, n_kz,
    point_maps, point_coils, direction_maps, direction_coils,
    residual_maps, residual_coils, inversion_times, sampling_mask,
):
    total = n_ti * n_kz
    coils = point_coils.shape[1]
    per_group = coils // COIL_GROUPS
    rows, ny = point_maps.shape[2:]
    width = ny // n_ti
    local_bins, nz, _ = sampling_mask.shape
    f32 = jnp.float32
    vmem = pl.BlockSpec(memory_space=pltpu.VMEM)
    dma = pltpu.SemaphoreType.DMA
    hbm = pl.BlockSpec(memory_space=pltpu.HBM)
    tables = [jnp.asarray(t) for t in (tables_y(ny), tables_z(nz))]
    flipped = [
        jnp.swapaxes(a, -1, -2) for a in (direction_maps, direction_coils, residual_maps, residual_coils)
    ]
    two, three = (lane_spans(rows, planes, width)[0] for planes in (2, 3))
    spots = (n_ti // COIL_GROUPS) * n_kz
    x_maps = pltpu.VMEM((COIL_GROUPS, spots, three, LANES), f32)
    y_maps = pltpu.VMEM((spots, three, LANES), f32)

    outs = pl.pallas_call(
        functools.partial(step_kernel, n_ti, n_kz, per_group),
        out_shape=[jax.ShapeDtypeStruct(shape, f32) for shape in (flipped[0].shape, flipped[1].shape, (2, 8, LANES))],
        in_specs=[hbm] * 6 + [pl.BlockSpec(memory_space=pltpu.SMEM)] + [hbm] * 3,
        out_specs=[vmem] * 3,
        scratch_shapes=[
            *(pltpu.VMEM(a.shape, f32) for a in flipped),
            pltpu.VMEM((local_bins, 8, LANES), f32),
            pltpu.VMEM((ny, ny), jnp.bfloat16),
            pltpu.VMEM((nz, nz), jnp.bfloat16),
            pltpu.VMEM((COIL_GROUPS, nz, 2 * ny), f32),
            *(pltpu.VMEM(t.shape, f32) for t in tables),
            pltpu.VMEM((n_kz, COIL_GROUPS, two, LANES), f32),
            pltpu.VMEM((n_kz, COIL_GROUPS, two, LANES), f32),
            pltpu.VMEM((total, two, LANES), f32),
            pltpu.VMEM((total, two, LANES), f32),
            pltpu.VMEM((n_kz, 3, rows, ny), f32),
            pltpu.VMEM((n_kz, 2, per_group, rows, ny), f32),
            pltpu.VMEM((COIL_GROUPS, local_bins, 8, LANES), f32),
            pltpu.VMEM((COIL_GROUPS,) + sampling_mask.shape, jnp.int32),
            pltpu.VMEM((2, 2, 2, ny, ny), jnp.bfloat16),
            pltpu.VMEM((2, 2, 2 * nz, nz), jnp.bfloat16),
            pltpu.VMEM((3, nz, ny), f32),
            pltpu.VMEM((2 * per_group, nz, ny), f32),
            pltpu.VMEM((3, nz, ny), f32),
            pltpu.VMEM((2 * per_group, nz, ny), f32),
            pltpu.VMEM((3, nz, ny), f32),
            pltpu.VMEM((2 * per_group, nz, ny), f32),
            pltpu.VMEM((total, two, LANES), f32),
            pltpu.VMEM((total, two, LANES), f32),
            pltpu.VMEM((total, two, LANES), f32),
            pltpu.VMEM((total, two, LANES), f32),
            pltpu.VMEM((8, LANES), f32),
            pltpu.VMEM((total, 8, LANES), f32),
            pltpu.VMEM((n_kz, three, LANES), f32),
            x_maps, x_maps, x_maps, y_maps, y_maps,
        ]
        + [dma] * 10
        + [dma((spots,))] * 4
        + [dma((COIL_GROUPS,))] * 4
        + [dma((n_kz,))] * 4
        + [dma((COIL_GROUPS,))] * 6
        + [dma((9,))],
        compiler_params=pltpu.CompilerParams(
            collective_id=0, has_side_effects=True, vmem_limit_bytes=VMEM_LIMIT
        ),
        name="step",
    )(*flipped, point_maps, point_coils, inversion_times, sampling_mask, *tables)
    updated = pl.pallas_call(
        finish_kernel,
        out_shape=[jax.ShapeDtypeStruct(flipped[i].shape, f32) for i in (0, 1, 0, 1)],
        in_specs=[vmem] * 7,
        out_specs=[vmem] * 4,
        compiler_params=pltpu.CompilerParams(vmem_limit_bytes=16 * 1024 * 1024),
        name="finish",
    )(outs[2], outs[0], outs[1], *flipped)
    return tuple(jnp.swapaxes(a, -1, -2) for a in updated)


def solution(mesh):
    in_specs = (
        P(None, None, "kz", None),
        P(None, None, None, "kz", None),
        P(None, None, "kz", "ti"),
        P(None, None, None, "kz", "ti"),
        P(None, None, "kz", "ti"),
        P(None, None, None, "kz", "ti"),
        P("ti"),
        P("ti", None, None),
    )
    out_specs = (
        P(None, None, "kz", "ti"),
        P(None, None, None, "kz", "ti"),
        P(None, None, "kz", "ti"),
        P(None, None, None, "kz", "ti"),
    )
    body = functools.partial(shards, mesh.shape["ti"], mesh.shape["kz"])
    return jax.shard_map(body, mesh=mesh, in_specs=in_specs, out_specs=out_specs, check_vma=False)
```

```python
import functools
import math

import jax
import jax.numpy as jnp
import numpy as np
from jax import lax
from jax.experimental import pallas as pl
from jax.experimental.pallas import tpu as pltpu
from jax.sharding import PartitionSpec as P

MESH = pl.DeviceIdType.MESH
regular_weight = 2.0
COIL_GROUPS = 4
LANES = 128
VMEM_LIMIT = 59 * 1024 * 1024


def half_parts(length, parity):
    points = np.arange(length // 2)
    orders = 2 * points + parity
    angles = (points[:, None] * orders[None, :] % length) * (2.0 * math.pi / length)
    factor = 1.0 / math.sqrt(length)
    return np.cos(angles) * factor, np.sin(angles) * factor


def tables_y(length):
    forward, backward = [], []
    for parity in range(2):
        c, s = half_parts(length, parity)
        forward.append(np.block([[c, -s], [s, c]]))
        backward.append(np.block([[c.T, s.T], [-s.T, c.T]]))
    return np.stack([np.stack(forward), np.stack(backward)]).astype(np.float32)


def tables_z(length):
    forward, backward = [], []
    for parity in range(2):
        c, s = half_parts(length, parity)
        forward.append(np.block([[c.T, s.T], [-s.T, c.T]]))
        backward.append(np.block([[c, -s], [s, c]]))
    return np.stack([np.stack(forward), np.stack(backward)]).astype(np.float32)


def even_then_odd(length, source_axis):
    source = lax.broadcasted_iota(jnp.int32, (length, length), source_axis)
    place = lax.broadcasted_iota(jnp.int32, (length, length), 1 - source_axis)
    wanted = jnp.where(place < length // 2, 2 * place, 2 * place - length + 1)
    return jnp.where(source == wanted, 1.0, 0.0).astype(jnp.bfloat16)


def halves(values):
    high = values.astype(jnp.bfloat16)
    low = (values - high.astype(jnp.float32)).astype(jnp.bfloat16)
    return high, low


dot = functools.partial(jnp.dot, preferred_element_type=jnp.float32)


def from_right(values, table):
    high, low = halves(values)
    return dot(high, table[0]) + (dot(low, table[0]) + dot(high, table[1]))


def from_left(table, values):
    high, low = halves(values)
    size = table.shape[1]
    both = dot(table, high)
    return both[:size] + (both[size:] + dot(table[:size], low))


def lane_spans(rows, planes, width):
    count = LANES // (planes * width)
    chunk = -(-(-(-rows // count)) // 8) * 8
    return chunk, [(start, min(chunk, rows - start)) for start in range(0, rows, chunk)]


def lane_blocks(rows, width):
    return lax.broadcasted_iota(jnp.int32, (rows, LANES), 1) // width


def turned(values, shift):
    shift %= LANES
    return pltpu.roll(values, shift, 1) if shift else values


def tall(values, rows):
    missing = rows - values.shape[0]
    if missing:
        values = jnp.concatenate([values, jnp.zeros((missing,) + values.shape[1:], values.dtype)], axis=0)
    return values


def fold(parts, width):
    rows = parts[0].shape[1]
    planes = len(parts)
    chunk, spans = lane_spans(rows, planes, width)
    block = tall(jnp.concatenate(parts, axis=0), LANES).T
    if len(spans) == 1:
        return tall(block, chunk)
    ids = lane_blocks(chunk, planes * width)
    value = jnp.zeros((chunk, LANES), jnp.float32)
    for i, (start, size) in enumerate(spans):
        moved = turned(tall(block[start : start + size], chunk), i * planes * width)
        value = jnp.where(ids == i, moved, value)
    return value


def unfold(block, planes, rows, width):
    _, spans = lane_spans(rows, planes, width)
    parts = [turned(block[:size], -i * planes * width) for i, (_, size) in enumerate(spans)]
    return (jnp.concatenate(parts, axis=0) if len(parts) > 1 else parts[0]).T


def scatter_lanes(blocks, planes, rows, width, store):
    _, spans = lane_spans(rows, planes, width)
    for p in range(planes):
        for i, (start, size) in enumerate(spans):
            ids = lane_blocks(size, width)
            value = None
            for j, block in enumerate(blocks):
                moved = turned(block[:size], (j - i * planes - p) * width)
                value = moved if value is None else jnp.where(ids == j, moved, value)
            store(p, slice(start, start + size), value)


def collect_lanes(planes, j, rows, width):
    chunk, spans = lane_spans(rows, len(planes), width)
    ids = lane_blocks(chunk, width)
    value = jnp.zeros((chunk, LANES), jnp.float32)
    for p, plane in enumerate(planes):
        for i, (start, size) in enumerate(spans):
            q = i * len(planes) + p
            moved = turned(tall(plane[start : start + size], chunk), (q - j) * width)
            value = jnp.where(ids == q, moved, value)
    return value


def step_kernel(
    n_ti, n_kz, per_group,
    dir_maps_in, dir_coils_in, res_maps_in, res_coils_in, maps, coils, bin_times, mask,
    tables_y_in, tables_z_in,
    app_maps, app_coils, scales,
    dir_maps, dir_coils, res_maps, res_coils, times, order_y, order_z, kept_masks, wide_y, wide_z,
    send_a, send_b, got_a, got_b, got_maps, got_coils, got_times, got_mask, ytab, ztab,
    p_maps, p_coils, s_maps, s_coils, g_maps, g_coils,
    back_a, back_b, ret_a, ret_b, sums, got_sums,
    send_m, got_m, back_m, part_m, total_m, ret_m,
    a_out, a_in, b_out, b_in, ra_out, ra_in, rb_out, rb_in, sum_out, sum_in,
    m_out, m_in, rm_out, rm_in, fm_out, fm_in, pm_out, pm_in,
    map_out, map_in, coil_out, coil_in, time_out, time_in, mask_out, mask_in, pair_out, pair_in, own,
):
    total = n_ti * n_kz
    ti = lax.axis_index("ti")
    kz = lax.axis_index("kz")
    me = ti * n_kz + kz
    group = lax.rem(ti, COIL_GROUPS)
    half = ti // COIL_GROUPS
    n_half = n_ti // COIL_GROUPS
    first = half * COIL_GROUPS
    spot = half * n_kz + kz
    core = lax.rem(kz, 2)
    pair = kz + 1 - 2 * core
    width = dir_maps.shape[2]
    rows = dir_maps.shape[3]
    nz, ny = mask.shape[1:]
    tiles = ny // LANES
    per_tile = LANES // width
    my_coils = pl.ds(group * per_group, per_group)

    early = [
        pltpu.make_async_copy(dir_maps_in, dir_maps, own.at[6]),
        pltpu.make_async_copy(dir_coils_in, dir_coils, own.at[7]),
    ]
    for copy in early:
        copy.start()

    barrier = pltpu.get_barrier_semaphore()

    def greet(offset, carry):
        other = lax.rem(me + offset, total)
        pl.semaphore_signal(
            barrier, inc=1, device_id=(other // n_kz, lax.rem(other, n_kz)), device_id_type=MESH
        )
        return carry

    lax.fori_loop(1, total, greet, 0)

    locals_ = [
        pltpu.make_async_copy(maps.at[:, kz], got_maps.at[kz], own.at[0]),
        pltpu.make_async_copy(coils.at[:, my_coils, kz], got_coils.at[kz], own.at[1]),
        pltpu.make_async_copy(mask, got_mask.at[group], own.at[3]),
        pltpu.make_async_copy(tables_y_in, wide_y, own.at[4]),
        pltpu.make_async_copy(tables_z_in, wide_z, own.at[5]),
        pltpu.make_async_copy(res_maps_in, res_maps, own.at[2]),
        pltpu.make_async_copy(res_coils_in, res_coils, own.at[8]),
    ]
    for copy in locals_:
        copy.start()
    for b in range(2):
        times[b] = jnp.full((8, LANES), bin_times[b], jnp.float32)
        got_times[group, b] = jnp.full((8, LANES), bin_times[b], jnp.float32)
    for copy in early:
        copy.wait()

    for x in range(n_kz):
        send_m[x] = fold([dir_maps[m, x] for m in range(3)], width)
        for g in range(COIL_GROUPS):
            c = g * per_group
            send_a[x, g] = fold([dir_coils[0, c, x], dir_coils[1, c, x]], width)
    got_a[me] = send_a[kz, group]
    got_m[group, spot] = send_m[kz]

    pl.semaphore_wait(barrier, total - 1)

    def remote(src, dst, out_sem, in_sem, where):
        return pltpu.make_async_remote_copy(src, dst, out_sem, in_sem, device_id=where, device_id_type=MESH)

    def split_id(other):
        return other // n_kz, lax.rem(other, n_kz)

    def a_copy(other, slot):
        t, k = split_id(other)
        return remote(send_a.at[k, lax.rem(t, COIL_GROUPS)], got_a.at[slot], a_out, a_in, (t, k))

    def b_copy(other, slot):
        t, k = split_id(other)
        return remote(send_b.at[k, lax.rem(t, COIL_GROUPS)], got_b.at[slot], b_out, b_in, (t, k))

    def ra_copy(other, slot):
        return remote(back_a.at[other], ret_a.at[slot], ra_out, ra_in, split_id(other))

    def rb_copy(other, slot):
        return remote(back_b.at[other], ret_b.at[slot], rb_out, rb_in, split_id(other))

    def sum_copy(other, slot):
        return remote(sums, got_sums.at[slot], sum_out, sum_in, split_id(other))

    def send_all(copy):
        def body(offset, carry):
            copy(lax.rem(me + offset, total), me).start()
            return carry

        lax.fori_loop(1, total, body, 0)

    def wait_bytes(slots, sem):
        part = slots.at[pl.ds(0, total - 1)]
        pltpu.make_async_copy(part, part, sem).wait()

    def point_copies(other, slot):
        return [
            remote(maps.at[:, other], got_maps.at[slot], map_out.at[other], map_in.at[slot], (ti, other)),
            remote(coils.at[:, my_coils, other], got_coils.at[slot], coil_out.at[other], coil_in.at[slot], (ti, other)),
        ]

    def bin_copies(other, slot):
        where = (first + other, kz)
        return [
            remote(times, got_times.at[slot], time_out.at[other], time_in.at[slot], where),
            remote(mask.at[core], got_mask.at[slot, core], mask_out.at[other], mask_in.at[slot], where),
        ]

    def pair_copy(slot, plane):
        where = (ti, pair)
        return remote(got_mask.at[slot, plane], got_mask.at[slot, plane], pair_out.at[slot], pair_in.at[slot], where)

    def m_copy(other, slot):
        h, k = split_id(other)
        where = (h * COIL_GROUPS + group, k)
        return remote(send_m.at[k], got_m.at[group, slot], m_out.at[other], m_in.at[slot], where)

    def rm_copy(other, slot):
        h, k = split_id(other)
        where = (h * COIL_GROUPS + group, k)
        return remote(total_m.at[other], ret_m.at[slot], rm_out.at[other], rm_in.at[slot], where)

    def fm_copy(other, slot):
        return remote(got_m.at[slot], got_m.at[slot], fm_out.at[other], fm_in.at[slot], (first + other, kz))

    def pm_copy(other, slot):
        return remote(back_m.at[other], part_m.at[slot], pm_out.at[other], pm_in.at[slot], (first + other, kz))

    spots = n_half * n_kz
    for offset in range(1, spots):
        m_copy(lax.rem(spot + offset, spots), spot).start()
    send_all(a_copy)
    for offset in range(1, n_kz):
        for copy in point_copies(lax.rem(kz + offset, n_kz), kz):
            copy.start()
    for x in range(n_kz):
        for g in range(COIL_GROUPS):
            c = g * per_group + 1
            send_b[x, g] = fold([dir_coils[0, c, x], dir_coils[1, c, x]], width)
    got_b[me] = send_b[kz, group]
    for offset in range(1, spots):
        other = lax.rem(spot + offset, spots)
        m_copy(other, other).wait_send()
        m_copy(other, other).wait_recv()
    for offset in range(1, COIL_GROUPS):
        fm_copy(lax.rem(group + offset, COIL_GROUPS), group).start()
    for offset in range(1, COIL_GROUPS):
        for copy in bin_copies(lax.rem(group + offset, COIL_GROUPS), group):
            copy.start()
    send_all(b_copy)

    for copy in locals_:
        copy.wait()
    order_y[...] = even_then_odd(ny, 0)
    order_z[...] = even_then_odd(nz, 1)
    for way in range(2):
        for parity in range(2):
            high, low = halves(wide_y[way, parity])
            ytab[way, parity, 0] = high
            ytab[way, parity, 1] = low
            high, low = halves(wide_z[way, parity])
            ztab[way, parity, :nz] = high
            ztab[way, parity, nz:] = low
    for offset in range(1, n_kz):
        other = lax.rem(kz + offset, n_kz)
        for copy in point_copies(other, other):
            copy.wait_send()
            copy.wait_recv()
    for k in range(n_kz):
        span = slice(k * rows, (k + 1) * rows)
        for m in range(3):
            p_maps[m, span, :] = got_maps[k, m]
        for c in range(per_group):
            for ri in range(2):
                p_coils[2 * c + ri, span, :] = got_coils[k, ri, c]
    wait_bytes(got_a, a_in)
    for offset in range(1, COIL_GROUPS):
        other = lax.rem(group + offset, COIL_GROUPS)
        fm_copy(other, group).wait_send()
        fm_copy(other, other).wait_recv()

    def store_to(targets, k, h):
        def store(p, span, value):
            ref, plane = targets[p]
            ref[plane, k * rows + span.start : k * rows + span.stop, h * LANES : (h + 1) * LANES] = value

        return store

    coil_zero = [(s_coils, 0), (s_coils, 1)]
    coil_one = [(s_coils, 2), (s_coils, 3)]
    for k in range(n_kz):
        for h in range(tiles):
            sources = [(h * per_tile + j) * n_kz + k for j in range(per_tile)]
            scatter_lanes([got_a[s] for s in sources], 2, rows, width, store_to(coil_zero, k, h))
            parts_m = []
            for j in range(per_tile):
                t = h * per_tile + j
                parts_m.append(got_m[t % COIL_GROUPS, (t // COIL_GROUPS) * n_kz + k])
            scatter_lanes(parts_m, 3, rows, width, store_to([(s_maps, m) for m in range(3)], k, h))

    g_maps[...] = jnp.zeros_like(g_maps)
    g_coils[...] = jnp.zeros_like(g_coils)

    def coil_pass(c):
        def body(offset, carry):
            other = lax.rem(group + offset, COIL_GROUPS)
            if c == 0:
                if not isinstance(offset, int):
                    pair_copy(other, core).wait_send()
                    pair_copy(other, 1 - core).wait_recv()
                bits = jnp.concatenate([got_mask[other, 0], got_mask[other, 1]], axis=0)
                bits = dot(bits.astype(jnp.float32).astype(jnp.bfloat16), order_y[...])
                bits = jnp.concatenate([bits[:nz], bits[nz:]], axis=1).astype(jnp.bfloat16)
                kept_masks[other] = dot(order_z[...], bits)

            amplitude = p_maps[1]
            model = []
            rows_in = []
            for b in range(2):
                tau = got_times[other, b, 0:1, 0:1]
                decays = jnp.exp(-tau * p_maps[2])
                signal = p_maps[0] - amplitude * decays
                slope = amplitude * tau * decays
                signal_step = s_maps[0] - s_maps[1] * decays + slope * s_maps[2]
                real = p_coils[2 * c] * signal_step + s_coils[2 * c] * signal
                imag = p_coils[2 * c + 1] * signal_step + s_coils[2 * c + 1] * signal
                rows_in.append(jnp.concatenate([real, imag], axis=1))
                model.append((decays, signal, slope))
            x = jnp.concatenate(rows_in, axis=0)
            h = ny // 2
            left, right = [jnp.concatenate([x[:, o : o + h], x[:, ny + o : ny + o + h]], axis=1) for o in (0, h)]
            even = from_right(left + right, ytab[0, 0])
            odd = from_right(left - right, ytab[0, 1])
            parts_z = []
            for o in (0, h):
                parts_z.append(
                    jnp.concatenate(
                        [
                            v
                            for b in range(2)
                            for v in (even[b * nz : (b + 1) * nz, o : o + h], odd[b * nz : (b + 1) * nz, o : o + h])
                        ],
                        axis=1,
                    )
                )
            q = nz // 2
            top = jnp.concatenate([v[:q] for v in parts_z], axis=0)
            bottom = jnp.concatenate([v[q:] for v in parts_z], axis=0)
            kept_even = kept_masks[other, :q]
            kept_odd = kept_masks[other, q:]
            even = from_left(ztab[0, 0], top + bottom) * jnp.concatenate([kept_even] * 2, axis=0)
            odd = from_left(ztab[0, 1], top - bottom) * jnp.concatenate([kept_odd] * 2, axis=0)
            even = from_left(ztab[1, 0], even)
            odd = from_left(ztab[1, 1], odd)
            top, bottom = even + odd, even - odd
            real = jnp.concatenate([top[:q], bottom[:q]], axis=0)
            imag = jnp.concatenate([top[q:], bottom[q:]], axis=0)
            even, odd = [
                jnp.concatenate(
                    [
                        jnp.concatenate([v[:, b * ny + o : b * ny + o + h] for v in (real, imag)], axis=1)
                        for b in range(2)
                    ],
                    axis=0,
                )
                for o in (0, h)
            ]
            even = from_right(even, ytab[1, 0])
            odd = from_right(odd, ytab[1, 1])
            left, right = even + odd, even - odd
            for b, (decays, signal, slope) in enumerate(model):
                span = slice(b * nz, (b + 1) * nz)
                real = jnp.concatenate([left[span, :h], right[span, :h]], axis=1)
                imag = jnp.concatenate([left[span, h:], right[span, h:]], axis=1)
                projected = p_coils[2 * c] * real + p_coils[2 * c + 1] * imag
                g_coils[2 * c] += signal * real
                g_coils[2 * c + 1] += signal * imag
                g_maps[0] += projected
                g_maps[1] -= decays * projected
                g_maps[2] += slope * projected
            return carry

        if c == 0:
            body(0, 0)
            for offset in range(1, COIL_GROUPS):
                other = lax.rem(group + offset, COIL_GROUPS)
                for copy in bin_copies(other, other):
                    copy.wait_send()
                    copy.wait_recv()
                pair_copy(other, core).start()
            lax.fori_loop(1, COIL_GROUPS, body, 0)
        else:
            lax.fori_loop(0, COIL_GROUPS, body, 0)

    coil_pass(0)

    for k in range(n_kz):
        span = slice(k * rows, (k + 1) * rows)
        for h in range(tiles):
            lanes = slice(h * LANES, (h + 1) * LANES)
            planes = [g_coils[p, span, lanes] for p in range(2)]
            for j in range(per_tile):
                back_b[(h * per_tile + j) * n_kz + k] = collect_lanes(planes, j, rows, width)
    send_all(rb_copy)
    ret_b[me] = back_b[me]

    wait_bytes(got_b, b_in)
    for k in range(n_kz):
        for h in range(tiles):
            sources = [(h * per_tile + j) * n_kz + k for j in range(per_tile)]
            scatter_lanes([got_b[s] for s in sources], 2, rows, width, store_to(coil_one, k, h))

    coil_pass(1)

    for k in range(n_kz):
        span = slice(k * rows, (k + 1) * rows)
        for h in range(tiles):
            lanes = slice(h * LANES, (h + 1) * LANES)
            planes = [g_maps[m, span, lanes] for m in range(3)]
            for j in range(per_tile):
                t = h * per_tile + j
                back_m[t % COIL_GROUPS, (t // COIL_GROUPS) * n_kz + k] = collect_lanes(planes, j, rows, width)
    for offset in range(1, COIL_GROUPS):
        pm_copy(lax.rem(group + offset, COIL_GROUPS), group).start()
    for k in range(n_kz):
        span = slice(k * rows, (k + 1) * rows)
        for h in range(tiles):
            lanes = slice(h * LANES, (h + 1) * LANES)
            planes = [g_coils[p, span, lanes] for p in (2, 3)]
            for j in range(per_tile):
                back_a[(h * per_tile + j) * n_kz + k] = collect_lanes(planes, j, rows, width)
    send_all(ra_copy)
    ret_a[me] = back_a[me]
    others = [lax.rem(group + offset, COIL_GROUPS) for offset in range(1, COIL_GROUPS)]
    for other in others:
        pm_copy(other, group).wait_send()
        pm_copy(other, other).wait_recv()
    total_m[...] = (back_m[group] + part_m[others[0]]) + (part_m[others[1]] + part_m[others[2]])
    for offset in range(1, spots):
        rm_copy(lax.rem(spot + offset, spots), spot).start()
    ret_m[spot] = total_m[spot]
    wait_bytes(ret_b, rb_in)

    parts = {"old": None, "bend": None, "cross": None, "square": None}

    def settle(applied, grad, d, r):
        a = grad + regular_weight * d
        for key, value in (("old", r * r), ("bend", d * a), ("cross", r * a), ("square", a * a)):
            parts[key] = value if parts[key] is None else parts[key] + value
        return a

    def settle_coils(c, x, flat):
        for ri in range(2):
            grad = flat[ri * width : (ri + 1) * width]
            app_coils[ri, c, x] = settle(None, grad, dir_coils[ri, c, x], res_coils[ri, c, x])

    def added(terms):
        return functools.reduce(lambda u, v: u + v, terms)

    for x in range(n_kz):
        for g in range(COIL_GROUPS):
            block = added([ret_b[t * n_kz + x] for t in range(g, n_ti, COIL_GROUPS)])
            settle_coils(g * per_group, x, unfold(block, 2, rows, width))

    wait_bytes(ret_a, ra_in)
    for x in range(n_kz):
        for g in range(COIL_GROUPS):
            block = added([ret_a[t * n_kz + x] for t in range(g, n_ti, COIL_GROUPS)])
            settle_coils(g * per_group + 1, x, unfold(block, 2, rows, width))
    for offset in range(1, spots):
        other = lax.rem(spot + offset, spots)
        rm_copy(other, other).wait_send()
        rm_copy(other, other).wait_recv()
    for x in range(n_kz):
        flat = unfold(added([ret_m[h * n_kz + x] for h in range(n_half)]), 3, rows, width)
        grads = [flat[m * width : (m + 1) * width] for m in range(3)]
        for m, grad in enumerate(grads):
            app_maps[m, x] = settle(None, grad, dir_maps[m, x], res_maps[m, x])

    row = lax.broadcasted_iota(jnp.int32, sums.shape, 0)
    tile = jnp.zeros(sums.shape, jnp.float32)
    for i, part in enumerate(parts.values()):
        tile = jnp.where(row == i, jnp.sum(part, keepdims=True), tile)
    sums[...] = tile
    send_all(sum_copy)
    got_sums[me] = tile
    wait_bytes(got_a, a_out)
    wait_bytes(got_b, b_out)
    wait_bytes(ret_a, ra_out)
    wait_bytes(ret_b, rb_out)
    wait_bytes(got_sums, sum_in)
    wait_bytes(got_sums, sum_out)
    whole = jnp.sum(got_sums[...], axis=0)
    old, bend, cross, square = (whole[i : i + 1, :] for i in range(4))
    step = old / bend
    ratio = (old - 2.0 * step * cross + step * step * square) / old
    scales[0] = jnp.broadcast_to(step, scales.shape[1:])
    scales[1] = jnp.broadcast_to(ratio, scales.shape[1:])


def finish_kernel(scales, app_maps, app_coils, dir_maps, dir_coils, res_maps, res_coils, *outs):
    step = scales[0, 0:1, 0 : app_maps.shape[-1]]
    ratio = scales[1, 0:1, 0 : app_maps.shape[-1]]
    for i, (applied, d, r) in enumerate(((app_maps, dir_maps, res_maps), (app_coils, dir_coils, res_coils))):
        updated = r[...] - step * applied[...]
        outs[i][...] = updated
        outs[2 + i][...] = updated + ratio * d[...]


def shards(
    n_ti, n_kz,
    point_maps, point_coils, direction_maps, direction_coils,
    residual_maps, residual_coils, inversion_times, sampling_mask,
):
    total = n_ti * n_kz
    coils = point_coils.shape[1]
    per_group = coils // COIL_GROUPS
    rows, ny = point_maps.shape[2:]
    width = ny // n_ti
    local_bins, nz, _ = sampling_mask.shape
    f32 = jnp.float32
    vmem = pl.BlockSpec(memory_space=pltpu.VMEM)
    dma = pltpu.SemaphoreType.DMA
    hbm = pl.BlockSpec(memory_space=pltpu.HBM)
    tables = [jnp.asarray(t) for t in (tables_y(ny), tables_z(nz))]
    flipped = [
        jnp.swapaxes(a, -1, -2) for a in (direction_maps, direction_coils, residual_maps, residual_coils)
    ]
    two, three = (lane_spans(rows, planes, width)[0] for planes in (2, 3))
    spots = (n_ti // COIL_GROUPS) * n_kz
    x_maps = pltpu.VMEM((COIL_GROUPS, spots, three, LANES), f32)
    y_maps = pltpu.VMEM((spots, three, LANES), f32)

    outs = pl.pallas_call(
        functools.partial(step_kernel, n_ti, n_kz, per_group),
        out_shape=[jax.ShapeDtypeStruct(shape, f32) for shape in (flipped[0].shape, flipped[1].shape, (2, 8, LANES))],
        in_specs=[hbm] * 6 + [pl.BlockSpec(memory_space=pltpu.SMEM)] + [hbm] * 3,
        out_specs=[vmem] * 3,
        scratch_shapes=[
            *(pltpu.VMEM(a.shape, f32) for a in flipped),
            pltpu.VMEM((local_bins, 8, LANES), f32),
            pltpu.VMEM((ny, ny), jnp.bfloat16),
            pltpu.VMEM((nz, nz), jnp.bfloat16),
            pltpu.VMEM((COIL_GROUPS, nz, 2 * ny), f32),
            *(pltpu.VMEM(t.shape, f32) for t in tables),
            pltpu.VMEM((n_kz, COIL_GROUPS, two, LANES), f32),
            pltpu.VMEM((n_kz, COIL_GROUPS, two, LANES), f32),
            pltpu.VMEM((total, two, LANES), f32),
            pltpu.VMEM((total, two, LANES), f32),
            pltpu.VMEM((n_kz, 3, rows, ny), f32),
            pltpu.VMEM((n_kz, 2, per_group, rows, ny), f32),
            pltpu.VMEM((COIL_GROUPS, local_bins, 8, LANES), f32),
            pltpu.VMEM((COIL_GROUPS,) + sampling_mask.shape, jnp.int32),
            pltpu.VMEM((2, 2, 2, ny, ny), jnp.bfloat16),
            pltpu.VMEM((2, 2, 2 * nz, nz), jnp.bfloat16),
            pltpu.VMEM((3, nz, ny), f32),
            pltpu.VMEM((2 * per_group, nz, ny), f32),
            pltpu.VMEM((3, nz, ny), f32),
            pltpu.VMEM((2 * per_group, nz, ny), f32),
            pltpu.VMEM((3, nz, ny), f32),
            pltpu.VMEM((2 * per_group, nz, ny), f32),
            pltpu.VMEM((total, two, LANES), f32),
            pltpu.VMEM((total, two, LANES), f32),
            pltpu.VMEM((total, two, LANES), f32),
            pltpu.VMEM((total, two, LANES), f32),
            pltpu.VMEM((8, LANES), f32),
            pltpu.VMEM((total, 8, LANES), f32),
            pltpu.VMEM((n_kz, three, LANES), f32),
            x_maps, x_maps, x_maps, y_maps, y_maps,
        ]
        + [dma] * 10
        + [dma((spots,))] * 4
        + [dma((COIL_GROUPS,))] * 4
        + [dma((n_kz,))] * 4
        + [dma((COIL_GROUPS,))] * 6
        + [dma((9,))],
        compiler_params=pltpu.CompilerParams(
            collective_id=0, has_side_effects=True, vmem_limit_bytes=VMEM_LIMIT
        ),
        name="step",
    )(*flipped, point_maps, point_coils, inversion_times, sampling_mask, *tables)
    def whole(array):
        return pl.BlockSpec(array.shape, lambda i: (0,) * array.ndim)

    updated = pl.pallas_call(
        finish_kernel,
        out_shape=[jax.ShapeDtypeStruct(flipped[i].shape, f32) for i in (0, 1, 0, 1)],
        grid=(1,),
        in_specs=[whole(outs[2]), whole(outs[0]), whole(outs[1])] + [vmem] * 4,
        out_specs=[whole(flipped[i]) for i in (0, 1, 0, 1)],
        compiler_params=pltpu.CompilerParams(vmem_limit_bytes=61 * 1024 * 1024),
        name="finish",
    )(outs[2], outs[0], outs[1], *flipped)
    return tuple(jnp.swapaxes(a, -1, -2) for a in updated)


def solution(mesh):
    in_specs = (
        P(None, None, "kz", None),
        P(None, None, None, "kz", None),
        P(None, None, "kz", "ti"),
        P(None, None, None, "kz", "ti"),
        P(None, None, "kz", "ti"),
        P(None, None, None, "kz", "ti"),
        P("ti"),
        P("ti", None, None),
    )
    out_specs = (
        P(None, None, "kz", "ti"),
        P(None, None, None, "kz", "ti"),
        P(None, None, "kz", "ti"),
        P(None, None, None, "kz", "ti"),
    )
    body = functools.partial(shards, mesh.shape["ti"], mesh.shape["kz"])
    return jax.shard_map(body, mesh=mesh, in_specs=in_specs, out_specs=out_specs, check_vma=False)
```
